128 devices in a mesh: dom: 4 (over x), sub: 32 (over z, y, core).
Axes of the slice: x: 4, y: 4, z: 4, core: 2. Of those that a mesh axis runs over, the one named last changes fastest.
Arguments:
- history: float32 [4, 192, 32768], P(None, None, ('dom', 'sub')), may hold values from -1.5 to 1.5
- diag_blocks: bfloat16 [1152, 32768], P(None, ('dom', 'sub')), may hold values from -1.25 to 1.25
- pair_blocks: bfloat16 [1152, 393216], P(None, ('dom', 'sub')), may hold values from -0.25 to 0.25
- neighbours: int32 [393216], P(('dom', 'sub')), may hold values from 0 to 32767, as said below
- counts: int32 [128], P(('dom', 'sub')), may hold values from 64 to 256, as said below
Outputs:
- products: float32 [384, 32768], P(None, ('dom', 'sub'))
- pair_scores: float32 [128, 393216], P(None, ('dom', 'sub'))
The draws below stay inside these ranges and needn't reach their ends.
Inputs may be any that keep to these rules, and one draw needn't show every extreme that they name: `neighbours`: entry p of the device block of 3072 entries belongs to that device's molecule slot p // 12. Every entry names a live molecule of a device whose dom index differs from the entry's own device's by at most one, periodically, with any sub index. Of one device's block, at most 64 entries name molecules of any one device, and some device is named exactly 64 times. `counts`: the live molecules of a device are its first count slots; some device holds 256.
All inputs are finite; a program needn't handle non-finite values.
Results may differ from the reference program's by a relative error of at most 0.006.
Values may be sent and summed in bfloat16 or wider, within the bound.
No kernel may reach another device: no remote copies, remote signals or barrier semaphores. Data moves between devices by JAX's collectives and lax.ppermute only.
A program may use at most 256 MiB of HBM per device.

```python
import jax
import jax.numpy as jnp
from jax import lax

BAS = 24
OCC = 8
HIST = 4
NB = 12
MOL_DEV = 256
MOLS = 32768
PAIRS = 393216
CAP = 64
N_DOM = 4
N_SUB = 32


def shared_counts(key):
    key = jax.random.fold_in(key, 11)
    first, second = jax.random.split(key)
    devices = N_DOM * N_SUB
    device = jnp.arange(devices)
    domain = device // N_SUB
    ramp = MOL_DEV // 4 + 3 * MOL_DEV // 4 * domain // (N_DOM - 1)
    jitter = jax.random.randint(first, (devices,), -(MOL_DEV // 8), MOL_DEV // 8 + 1)
    filled = jnp.clip(ramp + jitter, MOL_DEV // 4, MOL_DEV)
    fullest = jax.random.randint(second, (), 0, devices)
    return jnp.where(device == fullest, MOL_DEV, filled).astype(jnp.int32)


def draw_counts(key, part):
    return shared_counts(key)


def draw_neighbours(key, part):
    counts = shared_counts(key)
    key = jax.random.fold_in(key, 3)
    first, second, third = jax.random.split(key, 3)
    devices = N_DOM * N_SUB
    width = MOL_DEV * NB
    kinds = 3 * N_SUB
    bound = CAP
    favourite = jax.random.randint(first, (devices,), 0, kinds).astype(jnp.int32)
    listed = (jnp.arange(kinds * bound) // bound).astype(jnp.int32)

    def one_device(chosen, device_key):
        perm_key, mix_key = jax.random.split(device_key)
        shifted = (listed + chosen) % kinds
        others = shifted[bound:]
        picked = others[jax.random.permutation(perm_key, others.shape[0])][:width - bound]
        whole = jnp.concatenate([jnp.zeros((bound,), jnp.int32) + chosen, picked])
        return whole[jax.random.permutation(mix_key, width)]
    local = jax.vmap(one_device)(favourite, jax.random.split(second, devices)).reshape(-1)
    total = devices * width
    device = jnp.arange(total) // width
    domain = device // N_SUB
    offset = local // N_SUB
    region = local % N_SUB
    target = (domain + offset - 1) % N_DOM * N_SUB + region
    slot = jax.random.randint(third, (total,), 0, 1048576) % counts[target]
    return (target * MOL_DEV + slot).astype(jnp.int32)


def steps_of(own_key, dims, cuts, low, high):
    level = 1.0
    for axis_at, shards_of in cuts:
        steps = jax.random.uniform(jax.random.fold_in(jax.random.fold_in(own_key, 6), axis_at), (shards_of,), jnp.float32, low / len(cuts), high / len(cuts))
        level = level * jnp.repeat(jnp.exp(steps), dims[axis_at] // shards_of).reshape((-1,) + (1,) * (len(dims) - 1 - axis_at))
    return level


def scatter_about(stream_key, extent, scale, most, pieces=(), kind=jnp.bfloat16):
    gain = steps_of(stream_key, extent, pieces, -0.22, 0.18) if pieces else 1.0
    array = jax.random.normal(stream_key, extent, jnp.float32) * scale * gain
    return jnp.minimum(jnp.maximum(array, -most), most).astype(kind)


def setup_inputs(seed: int = 0) -> dict:
    splits = jax.random.split(jax.random.key(seed), 6)
    history = scatter_about(splits[0], (HIST, BAS * OCC, MOLS), 0.25, 1.5, ((2, 128),), jnp.float32)
    diag_blocks = scatter_about(splits[1], (2 * BAS * BAS, MOLS), BAS ** -0.5, 1.25, ((1, 128),))
    pair_blocks = scatter_about(splits[2], (2 * BAS * BAS, PAIRS), (2 * BAS * NB) ** -0.5, 0.25, ((1, 128),))
    neighbours = draw_neighbours(jax.random.fold_in(splits[5], 71), 0)
    counts = draw_counts(jax.random.fold_in(splits[5], 71), 0)
    return dict(history=history, diag_blocks=diag_blocks, pair_blocks=pair_blocks, neighbours=neighbours, counts=counts)


ASPC_WEIGHTS = (2.8, -2.8, 1.2, -0.2)


def predict(history):
    total = ASPC_WEIGHTS[0] * history[0]
    for level in range(1, 4):
        total = total + ASPC_WEIGHTS[level] * history[level]
    return total.astype(jnp.bfloat16)


def reference(history, diag_blocks, pair_blocks, neighbours, counts):
    guess = predict(history).astype(jnp.float32)
    width = MOL_DEV * NB
    devices = N_DOM * N_SUB
    rows = 2 * BAS * OCC
    highest = lax.Precision.HIGHEST

    def device_step(dev, carry):
        accum, scores = carry
        start = (dev * width).astype(jnp.int32)
        blocks = lax.dynamic_slice_in_dim(pair_blocks, start, width, 1).astype(jnp.float32).reshape(2, BAS, BAS, width)
        near = lax.dynamic_slice_in_dim(neighbours, start, width, 0).astype(jnp.int32)
        theirs = jnp.take(guess, near, axis=1).reshape(BAS, OCC, width)
        own_rows = lax.dynamic_slice_in_dim(guess, (dev * MOL_DEV).astype(jnp.int32), MOL_DEV, 1)
        mine = jnp.repeat(own_rows, NB, axis=1).reshape(BAS, OCC, width)
        live = (jnp.arange(width) // NB < counts[dev]).astype(jnp.float32)
        applied = jnp.einsum("cabp,blp->calp", blocks, theirs, precision=highest)
        reduced = jnp.einsum("akp,calp->cklp", mine, applied, precision=highest)
        turned = jnp.einsum("cabp,alp->cblp", blocks, mine, precision=highest)
        forward = (applied.reshape(rows, width) * live).reshape(rows, MOL_DEV, NB).sum(axis=2)
        accum = accum.at[:, near].add(turned.reshape(rows, width) * live)
        here = (dev * MOL_DEV).astype(jnp.int32)
        current = lax.dynamic_slice_in_dim(accum, here, MOL_DEV, 1)
        accum = lax.dynamic_update_slice_in_dim(accum, current + forward, here, 1)
        scores = lax.dynamic_update_slice_in_dim(scores, reduced.reshape(2 * OCC * OCC, width) * live, start, 1)
        return accum, scores

    accum = jnp.zeros((rows, MOLS), jnp.float32)
    scores = jnp.zeros((2 * OCC * OCC, PAIRS), jnp.float32)
    accum, scores = lax.fori_loop(0, devices, device_step, (accum, scores))
    square = diag_blocks.astype(jnp.float32).reshape(2, BAS, BAS, MOLS)
    local = jnp.einsum("cabm,blm->calm", square, guess.reshape(BAS, OCC, MOLS), precision=highest).reshape(rows, MOLS)
    slots = jnp.arange(MOLS)
    alive = (slots % MOL_DEV < counts[slots // MOL_DEV]).astype(jnp.float32)
    return (local + accum) * alive, scores
```

```python
import functools

import jax
import jax.numpy as jnp
from jax import lax
from jax.experimental import pallas as pl
from jax.experimental.pallas import tpu as pltpu
from jax.sharding import PartitionSpec as P

BAS = 24
OCC = 8
FEAT = BAS * OCC
ROWS = 2 * FEAT
CAP = 64
LANES = 128
SIDES = 3
ASPC_WEIGHTS = (2.8, -2.8, 1.2, -0.2)
VMEM = pl.BlockSpec(memory_space=pltpu.VMEM)
SMEM = pl.BlockSpec(memory_space=pltpu.SMEM)
NT = (((1,), (1,)), ((), ()))


def iota(shape, dim):
    return lax.broadcasted_iota(jnp.int32, shape, dim)


def prepare_kernel(teams, domains, info, history, near, guess, rows, dest, index, label):
    mols = guess.shape[1]
    total = ASPC_WEIGHTS[0] * history[0]
    for level in range(1, 4):
        total = total + ASPC_WEIGHTS[level] * history[level]
    rounded = total.astype(jnp.bfloat16)
    guess[...] = rounded
    wide = rounded.astype(jnp.float32)
    for part in range(mols // LANES):
        cut = slice(part * LANES, (part + 1) * LANES)
        rows[cut, :] = wide[:LANES, cut].T.astype(jnp.bfloat16)
    rest = jnp.concatenate([wide[LANES:, :LANES], wide[LANES:, LANES:]], axis=0)
    rows[mols:, :] = rest.T.astype(jnp.bfloat16)

    my_domain = info[0]
    parity = info[2]
    listed = near[...]
    owner = listed // mols
    slot = listed % mols
    team = owner % teams
    offset = (owner // teams - my_domain + 1 + domains) % domains
    base = (team * SIDES + offset) * rows.shape[0]
    index[0] = base + slot
    index[1] = base + mols + slot % LANES
    index[2] = slot // LANES
    place = team * (SIDES * CAP) + offset * CAP
    key = team * 8 + offset
    keys = teams * 8
    square = (LANES, 2 * LANES)
    before = ((iota(square, 0) < iota(square, 1)) | (iota(square, 1) >= LANES)).astype(jnp.bfloat16)
    which = iota((keys, LANES), 0)
    carry = jnp.zeros((keys, LANES), jnp.float32)
    names = jnp.zeros((keys, LANES), jnp.float32)
    for block in range(listed.shape[0]):
        hit = which == key[block : block + 1]
        ones = jnp.where(hit, 1.0, 0.0)
        sums = jnp.dot(ones.astype(jnp.bfloat16), before, preferred_element_type=jnp.float32)
        prior = sums[:, :LANES] + carry
        carry = carry + sums[:, LANES:]
        rank = jnp.sum(jnp.where(hit, prior, 0.0), axis=0, keepdims=True).astype(jnp.int32)
        dest[block : block + 1, :] = place[block : block + 1] + rank
        column = iota((LANES, LANES), 0) == rank + parity * CAP
        named = jnp.where(hit, slot[block : block + 1].astype(jnp.float32), 0.0)
        names = names + lax.dot_general(
            named.astype(jnp.bfloat16),
            column.astype(jnp.bfloat16),
            NT,
            preferred_element_type=jnp.float32,
        )
    label[...] = names


def spread(guess, first, per_mol, count):
    mols = guess.shape[1]
    mol = iota((mols, LANES), 0)
    pair = iota((mols, LANES), 1) + first
    table = (pair >= mol * per_mol) & (pair < (mol + 1) * per_mol) & (mol < count)
    return jnp.dot(
        guess[...], table.astype(jnp.bfloat16), preferred_element_type=jnp.float32
    )


def turned_kernel(per_mol, dest, info, guess, blocks, label, out, wide, mine, turned, slots):
    step = pl.program_id(0)
    teams = out.shape[0]
    width = SIDES * CAP

    @pl.when(step == 0)
    def _():
        def clear(team, _):
            start = pl.multiple_of(team * width, width)
            for part in range(3):
                slots[part, pl.ds(start, width), :] = jnp.zeros((width, LANES), jnp.float32)
            return 0

        lax.fori_loop(0, teams, clear, 0)

    wide[...] = blocks[...].astype(jnp.float32)
    mine[...] = spread(guess, step * LANES, per_mol, info[1])
    results = []
    for side in range(2):
        sums = [[None] * 3 for _ in range(OCC)]
        for inner in range(BAS):
            first = (side * BAS + inner) * BAS
            block = [wide[first + 8 * g : first + 8 * g + 8, :] for g in range(3)]
            for k in range(OCC):
                row = mine[inner * OCC + k : inner * OCC + k + 1, :]
                for g in range(3):
                    term = block[g] * row
                    sums[k][g] = term if inner == 0 else sums[k][g] + term
        results += [sums[k][g] for k in range(OCC) for g in range(3)]
    for part in range(3):
        turned[part] = jnp.concatenate(results[part * 16 : part * 16 + 16], axis=0).T

    def move(pair, _):
        at = dest[step, pair]
        for part in range(3):
            slots[part, pl.ds(at, 1), :] = turned[part, pl.ds(pair, 1), :]
        return 0

    lax.fori_loop(0, LANES, move, 0, unroll=16)

    @pl.when(step == pl.num_programs(0) - 1)
    def _():
        def finish(team, _):
            start = pl.multiple_of(team * width, width)
            for part in range(3):
                out[team, part * width : (part + 1) * width, :] = slots[
                    part, pl.ds(start, width), :
                ].astype(jnp.bfloat16)
            names = label[pl.ds(pl.multiple_of(team * 8, 8), 8), :]
            names = jnp.concatenate([names, jnp.zeros_like(names)], axis=0)
            out[team, 3 * width : 3 * width + 16, :] = names.astype(jnp.bfloat16)
            return 0

        lax.fori_loop(0, teams, finish, 0)


def apply_blocks(wide, theirs, applied, mine):
    other = [theirs[OCC * b : OCC * b + OCC, :] for b in range(BAS)]
    reduced = [[None] * OCC for _ in range(2)]
    for a in range(BAS):
        for side in range(2):
            first = (side * BAS + a) * BAS
            total = None
            for b in range(BAS):
                term = wide[first + b : first + b + 1, :] * other[b]
                total = term if total is None else total + term
            row = (side * BAS + a) * OCC
            applied[row : row + OCC, :] = total
            if mine is not None:
                for k in range(OCC):
                    term = mine[a * OCC + k : a * OCC + k + 1, :] * total
                    reduced[side][k] = term if a == 0 else reduced[side][k] + term
    return reduced


def diagonal_kernel(guess, blocks, out, wide, mine):
    wide[...] = blocks[...].astype(jnp.float32)
    mine[...] = guess[...].astype(jnp.float32)
    apply_blocks(wide, mine, out, None)


def pairs_kernel(
    per_mol, index, info, guess, blocks, half, local, table, scores, total,
    wide, mine, theirs, applied, near_a, near_b, held, stage, sems,
):
    step = pl.program_id(0)
    chunk = stage.shape[1]
    chunks = table.shape[0] // chunk
    mols = guess.shape[1]

    @pl.when(step == 0)
    def _():
        total[...] = local[...]

        def copy(at):
            return pltpu.make_async_copy(
                table.at[pl.ds(at * chunk, chunk), :], stage.at[at % 2], sems.at[at % 2]
            )

        copy(0).start()
        for at in range(chunks):
            if at + 1 < chunks:
                copy(at + 1).start()
            copy(at).wait()
            held[at * chunk : (at + 1) * chunk, :] = stage[at % 2].astype(jnp.float32)

    def pick(pair, _):
        near_a[pl.ds(pair, 1), :] = held[pl.ds(index[0, step, pair], 1), :]
        near_b[pl.ds(pair, 1), :] = held[pl.ds(index[1, step, pair], 1), :]
        return 0

    lax.fori_loop(0, LANES, pick, 0, unroll=16)
    theirs[:LANES, :] = near_a[...].T
    rest = near_b[...].T
    theirs[LANES:, :] = jnp.where(half[0] > 0, rest[FEAT - LANES :], rest[: FEAT - LANES])
    wide[...] = blocks[...].astype(jnp.float32)
    mine[...] = spread(guess, step * LANES, per_mol, info[1])
    reduced = apply_blocks(wide, theirs, applied, mine)
    scores[...] = jnp.concatenate(reduced[0] + reduced[1], axis=0)
    mol = iota((LANES, mols), 1)
    pair = iota((LANES, mols), 0) + step * LANES
    collapse = (pair >= mol * per_mol) & (pair < (mol + 1) * per_mol) & (mol < info[1])
    total[...] += jnp.dot(
        applied[...].astype(jnp.bfloat16),
        collapse.astype(jnp.bfloat16),
        preferred_element_type=jnp.float32,
    )


def collect_kernel(blocks, lower, here, upper, sums):
    step = pl.program_id(0)
    mols = here.shape[0]
    width = SIDES * CAP

    @pl.when(step == 0)
    def _():
        sums[...] = jnp.zeros_like(sums)

    mol = iota((mols, LANES), 0).astype(jnp.float32)
    names = [blocks[i, 3 * width : 3 * width + 16, :].astype(jnp.float32) for i in range(2)]
    first = iota((1, LANES), 1) < CAP
    for side in range(SIDES):
        name = jnp.where(first, names[0][side : side + 1], names[1][side : side + 1])
        hit = (mol == name).astype(jnp.bfloat16)
        for part in range(3):
            at = part * width + side * CAP
            values = jnp.concatenate([blocks[i, at : at + CAP, :] for i in range(2)], axis=0)
            sums[side, part] += jnp.dot(hit, values, preferred_element_type=jnp.float32)

    @pl.when(step == pl.num_programs(0) - 1)
    def _():
        for part in range(3):
            cut = slice(part * LANES, (part + 1) * LANES)
            lower[:, cut] = sums[0, part].astype(lower.dtype)
            here[:, cut] = sums[1, part]
            upper[:, cut] = sums[2, part].astype(upper.dtype)


def finish_kernel(info, total, here, from_lower, from_upper, out):
    mols = here.shape[0]
    back = here[...] + from_lower[...].astype(jnp.float32) + from_upper[...].astype(jnp.float32)
    high = back.astype(jnp.bfloat16)
    low = (back - high.astype(jnp.float32)).astype(jnp.bfloat16)
    row = iota((ROWS, ROWS), 0)
    column = iota((ROWS, ROWS), 1)
    turn = (column // FEAT) * FEAT + column % BAS * OCC + column % FEAT // BAS
    order = (row == turn).astype(jnp.bfloat16)
    returned = lax.dot_general(order, high, NT, preferred_element_type=jnp.float32)
    returned = returned + lax.dot_general(order, low, NT, preferred_element_type=jnp.float32)
    alive = iota((ROWS, mols), 1) < info[1]
    out[...] = jnp.where(alive, total[...] + returned, 0.0)


def shifted(block, axis, distance):
    devices = range(lax.axis_size(axis))
    route = [((i - distance) % len(devices), i) for i in devices]
    return lax.ppermute(block, axis, route)


def params(mib=48):
    return pltpu.CompilerParams(vmem_limit_bytes=mib * 1024 * 1024)


def on_device(history, diag_blocks, pair_blocks, neighbours, counts):
    mols = history.shape[2]
    pairs = pair_blocks.shape[1]
    per_mol = pairs // mols
    teams = lax.axis_size("sub")
    domains = lax.axis_size("dom")
    columns = pairs // LANES
    held_rows = mols * FEAT // LANES
    width = SIDES * CAP
    shape = jax.ShapeDtypeStruct
    f32, bf16, i32 = jnp.float32, jnp.bfloat16, jnp.int32
    info = jnp.stack([lax.axis_index("dom"), counts[0], lax.axis_index("sub") % 2]).astype(i32)
    guess, rows, dest, index, label = pl.pallas_call(
        functools.partial(prepare_kernel, teams, domains),
        out_shape=(
            shape((FEAT, mols), bf16),
            shape((held_rows, LANES), bf16),
            shape((columns, LANES), i32),
            shape((3, columns, LANES), i32),
            shape((teams * 8, LANES), f32),
        ),
        in_specs=[SMEM, VMEM, VMEM],
        out_specs=(VMEM,) * 5,
        compiler_params=params(),
        name="prepare",
    )(info, history, neighbours.reshape(columns, LANES))

    near = jnp.stack([shifted(rows, "dom", 1), rows, shifted(rows, "dom", -1)])
    table = lax.all_gather(near, "sub", axis=0, tiled=False)
    table = table.reshape(teams * SIDES * held_rows, LANES)

    payload = pl.pallas_call(
        functools.partial(turned_kernel, per_mol),
        grid=(columns,),
        out_shape=shape((teams, 3 * width + 16, LANES), bf16),
        in_specs=[
            SMEM,
            SMEM,
            pl.BlockSpec((FEAT, mols), lambda i: (0, 0)),
            pl.BlockSpec((6 * FEAT, LANES), lambda i: (0, i)),
            pl.BlockSpec((teams * 8, LANES), lambda i: (0, 0)),
        ],
        out_specs=pl.BlockSpec((teams, 3 * width + 16, LANES), lambda i: (0, 0, 0)),
        scratch_shapes=[
            pltpu.VMEM((6 * FEAT, LANES), f32),
            pltpu.VMEM((FEAT, LANES), f32),
            pltpu.VMEM((3, LANES, LANES), f32),
            pltpu.VMEM((3, teams * width, LANES), f32),
        ],
        compiler_params=params(),
        name="turned",
    )(dest, info, guess, pair_blocks, label)

    received = lax.all_to_all(payload, "sub", 0, 0, tiled=True)

    local = pl.pallas_call(
        diagonal_kernel,
        grid=(mols // LANES,),
        out_shape=shape((ROWS, mols), f32),
        in_specs=[
            pl.BlockSpec((FEAT, LANES), lambda i: (0, i)),
            pl.BlockSpec((6 * FEAT, LANES), lambda i: (0, i)),
        ],
        out_specs=pl.BlockSpec((ROWS, LANES), lambda i: (0, i)),
        scratch_shapes=[
            pltpu.VMEM((6 * FEAT, LANES), f32),
            pltpu.VMEM((FEAT, LANES), f32),
        ],
        compiler_params=params(),
        name="diagonal",
    )(guess, diag_blocks)

    chunk = held_rows * SIDES * 2
    scores, total = pl.pallas_call(
        functools.partial(pairs_kernel, per_mol),
        grid=(columns,),
        out_shape=(shape((ROWS // 3, pairs), f32), shape((ROWS, mols), f32)),
        in_specs=[
            SMEM,
            SMEM,
            pl.BlockSpec((FEAT, mols), lambda i: (0, 0)),
            pl.BlockSpec((6 * FEAT, LANES), lambda i: (0, i)),
            pl.BlockSpec((1, 1, LANES), lambda i: (i, 0, 0)),
            pl.BlockSpec((ROWS, mols), lambda i: (0, 0)),
            pl.BlockSpec(memory_space=pl.ANY),
        ],
        out_specs=(
            pl.BlockSpec((ROWS // 3, LANES), lambda i: (0, i)),
            pl.BlockSpec((ROWS, mols), lambda i: (0, 0)),
        ),
        scratch_shapes=[
            pltpu.VMEM((6 * FEAT, LANES), f32),
            pltpu.VMEM((FEAT, LANES), f32),
            pltpu.VMEM((FEAT, LANES), f32),
            pltpu.VMEM((ROWS, LANES), f32),
            pltpu.VMEM((LANES, LANES), f32),
            pltpu.VMEM((LANES, LANES), f32),
            pltpu.VMEM((teams * SIDES * held_rows, LANES), f32),
            pltpu.VMEM((2, chunk, LANES), bf16),
            pltpu.SemaphoreType.DMA((2,)),
        ],
        compiler_params=params(),
        name="pairs",
    )(index, info, guess, pair_blocks, index[2].reshape(columns, 1, LANES), local, table)

    whole = pl.BlockSpec((mols, ROWS), lambda i: (0, 0))
    lower, here, upper = pl.pallas_call(
        collect_kernel,
        grid=(teams // 2,),
        out_shape=(shape((mols, ROWS), bf16), shape((mols, ROWS), f32), shape((mols, ROWS), bf16)),
        in_specs=[pl.BlockSpec((2, 3 * width + 16, LANES), lambda i: (i, 0, 0))],
        out_specs=(whole,) * 3,
        scratch_shapes=[pltpu.VMEM((SIDES, 3, mols, LANES), f32)],
        compiler_params=params(),
        name="collect",
    )(received)

    products = pl.pallas_call(
        finish_kernel,
        out_shape=shape((ROWS, mols), f32),
        in_specs=[SMEM] + [VMEM] * 4,
        out_specs=VMEM,
        compiler_params=params(),
        name="finish",
    )(info, total, here, shifted(upper, "dom", 1), shifted(lower, "dom", -1))
    return products, scores


def solution(mesh):
    in_specs = (
        P(None, None, ("dom", "sub")),
        P(None, ("dom", "sub")),
        P(None, ("dom", "sub")),
        P(("dom", "sub")),
        P(("dom", "sub")),
    )
    out_specs = (P(None, ("dom", "sub")), P(None, ("dom", "sub")))
    return jax.shard_map(
        on_device, mesh=mesh, in_specs=in_specs, out_specs=out_specs, check_vma=False
    )
```

```python
import functools

import jax
import jax.numpy as jnp
from jax import lax
from jax.experimental import pallas as pl
from jax.experimental.pallas import tpu as pltpu
from jax.sharding import PartitionSpec as P

BAS = 24
OCC = 8
FEAT = BAS * OCC
ROWS = 2 * FEAT
CAP = 64
LANES = 128
BLOCK = 4 * LANES
BATCH = 64
SIDES = 3
RING = 4
KEYS = 4
ASPC_WEIGHTS = (2.8, -2.8, 1.2, -0.2)
VMEM = pl.BlockSpec(memory_space=pltpu.VMEM)
SMEM = pl.BlockSpec(memory_space=pltpu.SMEM)
NT = (((1,), (1,)), ((), ()))
WIDTH = SIDES * CAP
PACKED = CAP * FEAT // LANES


def iota(shape, dim):
    return lax.broadcasted_iota(jnp.int32, shape, dim)


def relative(team, me):
    z = (team // (2 * RING) - me // (2 * RING) + RING) % RING
    y = (team // 2 % RING - me // 2 % RING + RING) % RING
    return (team % 2 + me) % 2 * RING * RING + y * RING + z


def absolute(place, me):
    z = (place + me // (2 * RING)) % RING
    y = (place // RING + me // 2) % RING
    return (z * RING + y) * 2 + (place // (RING * RING) + me) % 2


def ahead(block, dz, dy, core):
    route = []
    for target in range(2 * RING * RING):
        z, y, c = target // (2 * RING), target // 2 % RING, target % 2
        source = ((z + dz) % RING * RING + (y + dy) % RING) * 2 + (c + core) % 2
        route.append((source, target))
    return lax.ppermute(block, "sub", route)


def predict_kernel(history, guess, rows):
    mols = guess.shape[1]
    total = ASPC_WEIGHTS[0] * history[0]
    for level in range(1, 4):
        total = total + ASPC_WEIGHTS[level] * history[level]
    rounded = total.astype(jnp.bfloat16)
    guess[...] = rounded
    wide = rounded.astype(jnp.float32)
    for part in range(mols // LANES):
        cut = slice(part * LANES, (part + 1) * LANES)
        rows[cut, :] = wide[:LANES, cut].T.astype(jnp.bfloat16)
    rest = jnp.concatenate([wide[LANES:, :LANES], wide[LANES:, LANES:]], axis=0)
    rows[mols:, :] = rest.T.astype(jnp.bfloat16)


def rank_kernel(
    teams, domains, mols, info, near, dest, first_rows, rest_rows, half, wanted, label
):
    my_domain = info[0]
    parity = info[2]
    listed = near[...]
    owner = listed // mols
    slot = listed % mols
    team = relative(owner % teams, info[3])
    offset = (owner // teams - my_domain + 1 + domains) % domains
    place = team * WIDTH + offset * CAP
    inside = offset == 1
    held_rows = mols * FEAT // LANES
    beyond = teams * held_rows + (offset // 2 * teams + team) * PACKED
    key = team * KEYS + offset
    keys = teams * KEYS
    square = (LANES, 2 * LANES)
    before = ((iota(square, 0) < iota(square, 1)) | (iota(square, 1) >= LANES)).astype(jnp.bfloat16)
    which = iota((keys, LANES), 0)
    carry = jnp.zeros((keys, LANES), jnp.float32)
    names = jnp.zeros((keys, LANES), jnp.float32)
    for block in range(listed.shape[0]):
        at = slice(block, block + 1)
        hit = which == key[at]
        ones = jnp.where(hit, 1.0, 0.0)
        sums = jnp.dot(ones.astype(jnp.bfloat16), before, preferred_element_type=jnp.float32)
        prior = sums[:, :LANES] + carry
        carry = carry + sums[:, LANES:]
        rank = jnp.sum(jnp.where(hit, prior, 0.0), axis=0, keepdims=True).astype(jnp.int32)
        dest[at, :] = place[at] + rank
        base = team[at] * held_rows
        first_rows[at, :] = jnp.where(inside[at], base + slot[at], beyond[at] + rank)
        rest_rows[at, :] = jnp.where(
            inside[at],
            base + mols + slot[at] % LANES,
            beyond[at] + CAP + rank % (CAP // 2),
        )
        half[at, :] = jnp.where(inside[at], slot[at] // LANES, rank // (CAP // 2))
        column = iota((LANES, LANES), 0) == rank
        named = jnp.where(hit, slot[at].astype(jnp.float32), 0.0)
        names = names + lax.dot_general(
            named.astype(jnp.bfloat16),
            column.astype(jnp.bfloat16),
            NT,
            preferred_element_type=jnp.float32,
        )
    wanted[...] = names.astype(jnp.int32)
    label[...] = jnp.where(parity == 1, pltpu.roll(names, CAP, 1), names)


def answer_kernel(from_lower, from_upper, same, other, to_lower, to_upper):
    count, held_rows = same.shape[:2]
    teams = 2 * count
    mols = held_rows * LANES // FEAT
    half = CAP // 2
    names = []
    for asked in (from_lower, from_upper):
        names.append(asked[...].astype(jnp.float32).T)
    low = iota((LANES, LANES), 1) < FEAT - LANES
    mol = iota((CAP, mols), 1).astype(jnp.float32)
    for team in range(teams):
        held, at = (same, team) if team < count else (other, team - count)
        packed = held[at, mols:, :].astype(jnp.float32)
        turned = pltpu.roll(packed, FEAT - LANES, 1)
        rest = jnp.concatenate([jnp.where(low, packed, turned), jnp.where(low, turned, packed)], axis=0)
        values = jnp.concatenate([held[at, :mols, :], rest.astype(jnp.bfloat16)], axis=1)
        hits = []
        for side in range(2):
            column = team * KEYS + 2 - 2 * side
            name = names[side][:CAP, column : column + 1]
            hits.append((name == mol).astype(jnp.bfloat16))
        found = jnp.dot(jnp.concatenate(hits, axis=0), values, preferred_element_type=jnp.float32)
        for side, out in enumerate((to_lower, to_upper)):
            mine = found[side * CAP : (side + 1) * CAP]
            out[team, :CAP, :] = mine[:, :LANES].astype(jnp.bfloat16)
            pair = jnp.where(low[:half], mine[:half, LANES:], mine[half:, LANES:])
            out[team, CAP:, :] = pair.astype(jnp.bfloat16)


def owners(mols, first, per_mol, count):
    mol = (iota((1, BLOCK), 1) + first) // per_mol
    mol = jnp.where(mol < count, mol, -1)
    return (iota((mols, BLOCK), 0) == mol).astype(jnp.bfloat16)


def turned_kernel(per_mol, dest, info, guess, blocks, label, out, wide, mine, turned, slots, stage, sems):
    step = pl.program_id(0)
    teams = out.shape[0]
    width = WIDTH

    @pl.when(step == 0)
    def _():
        def clear(team, _):
            start = pl.multiple_of(team * width, width)
            for part in range(3):
                slots[part, pl.ds(start, width), :] = jnp.zeros((width, LANES), jnp.float32)
            return 0

        lax.fori_loop(0, teams, clear, 0)

    table = owners(guess.shape[1], step * BLOCK, per_mol, info[1])
    mine[...] = jnp.dot(guess[...], table, preferred_element_type=jnp.float32)

    def column(at, _):
        cut = pl.ds(pl.multiple_of(at * LANES, LANES), LANES)
        wide[...] = blocks[:, cut].astype(jnp.float32)
        results = []
        for side in range(2):
            sums = [[None] * 3 for _ in range(OCC)]
            for inner in range(BAS):
                first = (side * BAS + inner) * BAS
                block = [wide[first + 8 * g : first + 8 * g + 8, :] for g in range(3)]
                for k in range(OCC):
                    row = mine[inner * OCC + k : inner * OCC + k + 1, cut]
                    for g in range(3):
                        term = block[g] * row
                        sums[k][g] = term if inner == 0 else sums[k][g] + term
            results += [sums[k][g] for k in range(OCC) for g in range(3)]
        for part in range(3):
            turned[part] = jnp.concatenate(results[part * 16 : part * 16 + 16], axis=0).T

        line = step * BLOCK + at * LANES

        def move(first, _):
            first = pl.multiple_of(first * BATCH, BATCH)
            places = [dest[line + first + i] for i in range(BATCH)]
            rows = [
                [turned[part, pl.ds(first + i, 1), :] for part in range(3)] for i in range(BATCH)
            ]
            for place, row in zip(places, rows):
                for part in range(3):
                    slots[part, pl.ds(place, 1), :] = row[part]
            return 0

        return lax.fori_loop(0, LANES // BATCH, move, 0)

    lax.fori_loop(0, BLOCK // LANES, column, 0)

    @pl.when(step == pl.num_programs(0) - 1)
    def _():
        def copy(team):
            return pltpu.make_async_copy(
                stage.at[team], out.at[absolute(team, info[3])], sems.at[team]
            )

        def finish(team, _):
            start = pl.multiple_of(team * width, width)
            for part in range(3):
                stage[team, part * width : (part + 1) * width, :] = slots[
                    part, pl.ds(start, width), :
                ].astype(jnp.bfloat16)
            names = label[pl.ds(pl.multiple_of(team // 2 * 8, 8), 8), :]
            names = jnp.where(team % 2 == 1, pltpu.roll(names, KEYS, 0), names)
            names = jnp.concatenate([names, jnp.zeros_like(names)], axis=0)
            stage[team, 3 * width :, :] = names.astype(jnp.bfloat16)
            copy(team).start()
            return 0

        def wait(team, _):
            copy(team).wait()
            return 0

        lax.fori_loop(0, teams, finish, 0)
        lax.fori_loop(0, teams, wait, 0)


def apply_blocks(wide, theirs, applied, mine, cut):
    other = [theirs[OCC * b : OCC * b + OCC, :] for b in range(BAS)]
    reduced = [[None] * OCC for _ in range(2)]
    for a in range(BAS):
        for side in range(2):
            first = (side * BAS + a) * BAS
            total = None
            for b in range(BAS):
                term = wide[first + b : first + b + 1, :] * other[b]
                total = term if total is None else total + term
            row = (side * BAS + a) * OCC
            applied[row : row + OCC, cut] = total
            if mine is not None:
                for k in range(OCC):
                    term = mine[a * OCC + k : a * OCC + k + 1, cut] * total
                    reduced[side][k] = term if a == 0 else reduced[side][k] + term
    return reduced


def diagonal_kernel(guess, blocks, out, wide, mine):
    wide[...] = blocks[...].astype(jnp.float32)
    mine[...] = guess[...].astype(jnp.float32)
    apply_blocks(wide, mine, out, None, slice(0, LANES))


def pairs_kernel(
    per_mol, first_rows, rest_rows, info, guess, blocks, half, local, same, other, lower, upper, scores, total,
    wide, mine, theirs, applied, near_a, near_b, held,
):
    step = pl.program_id(0)
    mols = guess.shape[1]

    @pl.when(step == 0)
    def _():
        total[...] = local[...]

        base = 0
        for source in (same, other, lower, upper):
            rows = source.shape[1]

            def widen(team, _):
                start = pl.multiple_of(base + team * rows, rows)
                held[pl.ds(start, rows), :] = source[team].astype(jnp.float32)
                return 0

            lax.fori_loop(0, source.shape[0], widen, 0)
            base += source.shape[0] * rows

    table = owners(mols, step * BLOCK, per_mol, info[1])
    mine[...] = jnp.dot(guess[...], table, preferred_element_type=jnp.float32)

    def column(at, _):
        cut = pl.ds(pl.multiple_of(at * LANES, LANES), LANES)
        line = step * (BLOCK // LANES) + at

        def pick(first, _):
            first = pl.multiple_of(first * BATCH, BATCH)
            for index, near in ((first_rows, near_a), (rest_rows, near_b)):
                places = [index[line * LANES + first + i] for i in range(BATCH)]
                rows = [held[pl.ds(place, 1), :] for place in places]
                near[pl.ds(first, BATCH), :] = jnp.concatenate(rows, axis=0)
            return 0

        lax.fori_loop(0, LANES // BATCH, pick, 0)
        theirs[:LANES, :] = near_a[...].T
        rest = near_b[...].T
        theirs[LANES:, :] = jnp.where(
            half[pl.ds(line, 1), :] > 0, rest[FEAT - LANES :], rest[: FEAT - LANES]
        )
        wide[...] = blocks[:, cut].astype(jnp.float32)
        reduced = apply_blocks(wide, theirs, applied, mine, cut)
        scores[:, cut] = jnp.concatenate(reduced[0] + reduced[1], axis=0)
        return 0

    lax.fori_loop(0, BLOCK // LANES, column, 0)
    total[...] += lax.dot_general(
        applied[...].astype(jnp.bfloat16), table, NT, preferred_element_type=jnp.float32
    )


def collect_kernel(blocks, lower, here, upper, sums):
    step = pl.program_id(0)
    mols = here.shape[0]
    group = blocks.shape[0]

    @pl.when(step == 0)
    def _():
        sums[...] = jnp.zeros_like(sums)

    mol = iota((mols, group * CAP), 0).astype(jnp.float32)
    first = iota((1, LANES), 1) < CAP
    labels = [blocks[i, 3 * WIDTH :, :].astype(jnp.float32) for i in range(group)]
    for side in range(SIDES):
        at = slice(side, side + 1)
        names = [jnp.where(first, labels[i][at], labels[i + 1][at]) for i in range(0, group, 2)]
        hit = (mol == jnp.concatenate(names, axis=1)).astype(jnp.bfloat16)
        values = []
        for part in range(3):
            row = part * WIDTH + side * CAP
            values.append(
                jnp.concatenate([blocks[i, row : row + CAP, :] for i in range(group)], axis=0)
            )
        sums[side] += jnp.dot(
            hit, jnp.concatenate(values, axis=1), preferred_element_type=jnp.float32
        )

    @pl.when(step == pl.num_programs(0) - 1)
    def _():
        for side, out in enumerate((lower, here, upper)):
            out[...] = sums[side].astype(out.dtype)


def finish_kernel(info, total, here, from_lower, from_upper, out):
    mols = here.shape[0]
    back = here[...] + from_lower[...].astype(jnp.float32) + from_upper[...].astype(jnp.float32)
    high = back.astype(jnp.bfloat16)
    low = (back - high.astype(jnp.float32)).astype(jnp.bfloat16)
    row = iota((ROWS, ROWS), 0)
    column = iota((ROWS, ROWS), 1)
    turn = (column // FEAT) * FEAT + column % BAS * OCC + column % FEAT // BAS
    order = (row == turn).astype(jnp.bfloat16)
    returned = lax.dot_general(order, high, NT, preferred_element_type=jnp.float32)
    returned = returned + lax.dot_general(order, low, NT, preferred_element_type=jnp.float32)
    alive = iota((ROWS, mols), 1) < info[1]
    out[...] = jnp.where(alive, total[...] + returned, 0.0)


def shifted(block, axis, distance):
    devices = range(lax.axis_size(axis))
    route = [((i - distance) % len(devices), i) for i in devices]
    return lax.ppermute(block, axis, route)


def params(mib=48):
    return pltpu.CompilerParams(vmem_limit_bytes=mib * 1024 * 1024)


def cost(us):
    return pl.CostEstimate(flops=0, transcendentals=0, bytes_accessed=us * 3_600_000)


def on_device(history, diag_blocks, pair_blocks, neighbours, counts):
    mols = history.shape[2]
    pairs = pair_blocks.shape[1]
    per_mol = pairs // mols
    teams = lax.axis_size("sub")
    domains = lax.axis_size("dom")
    columns = pairs // LANES
    held_rows = mols * FEAT // LANES
    shape = jax.ShapeDtypeStruct
    f32, bf16, i32 = jnp.float32, jnp.bfloat16, jnp.int32
    info = jnp.stack([lax.axis_index("dom"), counts[0], lax.axis_index("sub") % 2, lax.axis_index("sub")]).astype(i32)
    guess, rows = pl.pallas_call(
        predict_kernel,
        out_shape=(shape((FEAT, mols), bf16), shape((held_rows, LANES), bf16)),
        in_specs=[VMEM],
        out_specs=(VMEM,) * 2,
        compiler_params=params(),
        name="predict",
    )(history)

    table = shape((columns, LANES), i32)
    dest, first_rows, rest_rows, half, wanted, label = pl.pallas_call(
        functools.partial(rank_kernel, teams, domains, mols),
        out_shape=(table,) * 4 + (shape((teams * KEYS, LANES), i32), shape((teams * KEYS, LANES), f32)),
        in_specs=[SMEM, VMEM],
        out_specs=(VMEM,) * 6,
        compiler_params=params(),
        cost_estimate=cost(3),
        name="rank",
    )(info, neighbours.reshape(columns, LANES))
    dest, first_rows, rest_rows = (x.reshape(pairs) for x in (dest, first_rows, rest_rows))

    same = jnp.stack([rows] + [ahead(rows, z, 0, 0) for z in range(1, RING)])
    same, dest = lax.optimization_barrier((same, dest))
    same = jnp.concatenate([same] + [ahead(same, 0, y, 0) for y in range(1, RING)])
    asked_lower, asked_upper = shifted(wanted, "dom", 1), shifted(wanted, "dom", -1)

    payload = pl.pallas_call(
        functools.partial(turned_kernel, per_mol),
        grid=(pairs // BLOCK,),
        out_shape=shape((teams, 3 * WIDTH + 16, LANES), bf16),
        in_specs=[
            SMEM,
            SMEM,
            pl.BlockSpec((FEAT, mols), lambda i: (0, 0)),
            pl.BlockSpec((6 * FEAT, BLOCK), lambda i: (0, i)),
            pl.BlockSpec((teams * KEYS, LANES), lambda i: (0, 0)),
        ],
        out_specs=pl.BlockSpec(memory_space=pltpu.HBM),
        scratch_shapes=[
            pltpu.VMEM((6 * FEAT, LANES), f32),
            pltpu.VMEM((FEAT, BLOCK), f32),
            pltpu.VMEM((3, LANES, LANES), f32),
            pltpu.VMEM((3, teams * WIDTH, LANES), f32),
            pltpu.VMEM((teams, 3 * WIDTH + 16, LANES), bf16),
            pltpu.SemaphoreType.DMA((teams,)),
        ],
        compiler_params=params(60),
        cost_estimate=cost(25),
        name="turned",
    )(dest, info, guess, pair_blocks, label)

    payload, same = lax.optimization_barrier((payload, same))
    received = lax.all_to_all(payload, "sub", 0, 0, tiled=True)

    other = ahead(same, 0, 0, 1)
    to_lower, to_upper = pl.pallas_call(
        answer_kernel,
        out_shape=(shape((teams, PACKED, LANES), bf16),) * 2,
        in_specs=[VMEM] * 4,
        out_specs=(VMEM,) * 2,
        compiler_params=params(),
        name="answer",
    )(asked_lower, asked_upper, same, other)
    upper = shifted(to_lower, "dom", -1)
    lower = shifted(to_upper, "dom", 1)

    local = pl.pallas_call(
        diagonal_kernel,
        grid=(mols // LANES,),
        out_shape=shape((ROWS, mols), f32),
        in_specs=[
            pl.BlockSpec((FEAT, LANES), lambda i: (0, i)),
            pl.BlockSpec((6 * FEAT, LANES), lambda i: (0, i)),
        ],
        out_specs=pl.BlockSpec((ROWS, LANES), lambda i: (0, i)),
        scratch_shapes=[
            pltpu.VMEM((6 * FEAT, LANES), f32),
            pltpu.VMEM((FEAT, LANES), f32),
        ],
        compiler_params=params(),
        name="diagonal",
    )(guess, diag_blocks)

    scores, total = pl.pallas_call(
        functools.partial(pairs_kernel, per_mol),
        grid=(pairs // BLOCK,),
        out_shape=(shape((ROWS // 3, pairs), f32), shape((ROWS, mols), f32)),
        in_specs=[
            SMEM,
            SMEM,
            SMEM,
            pl.BlockSpec((FEAT, mols), lambda i: (0, 0)),
            pl.BlockSpec((6 * FEAT, BLOCK), lambda i: (0, i)),
            pl.BlockSpec((columns, LANES), lambda i: (0, 0)),
            pl.BlockSpec((ROWS, mols), lambda i: (0, 0)),
            pl.BlockSpec((teams // 2, held_rows, LANES), lambda i: (0, 0, 0)),
            pl.BlockSpec((teams // 2, held_rows, LANES), lambda i: (0, 0, 0)),
            pl.BlockSpec((teams, PACKED, LANES), lambda i: (0, 0, 0)),
            pl.BlockSpec((teams, PACKED, LANES), lambda i: (0, 0, 0)),
        ],
        out_specs=(
            pl.BlockSpec((ROWS // 3, BLOCK), lambda i: (0, i)),
            pl.BlockSpec((ROWS, mols), lambda i: (0, 0)),
        ),
        scratch_shapes=[
            pltpu.VMEM((6 * FEAT, LANES), f32),
            pltpu.VMEM((FEAT, BLOCK), f32),
            pltpu.VMEM((FEAT, LANES), f32),
            pltpu.VMEM((ROWS, BLOCK), f32),
            pltpu.VMEM((LANES, LANES), f32),
            pltpu.VMEM((LANES, LANES), f32),
            pltpu.VMEM((teams * (held_rows + 2 * PACKED), LANES), f32),
        ],
        compiler_params=params(),
        cost_estimate=cost(35),
        name="pairs",
    )(first_rows, rest_rows, info, guess, pair_blocks, half, local, same, other, lower, upper)

    received, total = lax.optimization_barrier((received, total))
    whole = pl.BlockSpec((mols, ROWS), lambda i: (0, 0))
    group = 8
    below, here, above = pl.pallas_call(
        collect_kernel,
        grid=(teams // group,),
        out_shape=(shape((mols, ROWS), bf16), shape((mols, ROWS), f32), shape((mols, ROWS), bf16)),
        in_specs=[pl.BlockSpec((group, 3 * WIDTH + 16, LANES), lambda i: (i, 0, 0))],
        out_specs=(whole,) * 3,
        scratch_shapes=[pltpu.VMEM((SIDES, mols, ROWS), f32)],
        compiler_params=params(),
        name="collect",
    )(received)
    from_lower, from_upper = shifted(above, "dom", 1), shifted(below, "dom", -1)

    products = pl.pallas_call(
        finish_kernel,
        out_shape=shape((ROWS, mols), f32),
        in_specs=[SMEM] + [VMEM] * 4,
        out_specs=VMEM,
        compiler_params=params(),
        name="finish",
    )(info, total, here, from_lower, from_upper)
    return products, scores


def solution(mesh):
    in_specs = (
        P(None, None, ("dom", "sub")),
        P(None, ("dom", "sub")),
        P(None, ("dom", "sub")),
        P(("dom", "sub")),
        P(("dom", "sub")),
    )
    out_specs = (P(None, ("dom", "sub")), P(None, ("dom", "sub")))
    return jax.shard_map(
        on_device, mesh=mesh, in_specs=in_specs, out_specs=out_specs, check_vma=False
    )
```

```python
import functools

import jax
import jax.numpy as jnp
from jax import lax
from jax.experimental import pallas as pl
from jax.experimental.pallas import tpu as pltpu
from jax.sharding import PartitionSpec as P

BAS = 24
OCC = 8
FEAT = BAS * OCC
ROWS = 2 * FEAT
CAP = 64
LANES = 128
BLOCK = 4 * LANES
MOVES = 16
SIDES = 3
CHIPS = 16
MAIN = 160
SPARE = SIDES * CAP - MAIN
TAILS = LANES // SPARE
KEYS = 4
ASPC_WEIGHTS = (2.8, -2.8, 1.2, -0.2)
VMEM = pl.BlockSpec(memory_space=pltpu.VMEM)
SMEM = pl.BlockSpec(memory_space=pltpu.SMEM)
NT = (((1,), (1,)), ((), ()))
WIDTH = SIDES * CAP
PACKED = CAP * FEAT // LANES


def iota(shape, dim):
    return lax.broadcasted_iota(jnp.int32, shape, dim)


def relative(team, me):
    return (team + me) % 2 * CHIPS + team // 2


def absolute(place, me):
    return place % CHIPS * 2 + (place // CHIPS + me) % 2


def predict_kernel(history, guess, rows):
    mols = guess.shape[1]
    total = ASPC_WEIGHTS[0] * history[0]
    for level in range(1, 4):
        total = total + ASPC_WEIGHTS[level] * history[level]
    rounded = total.astype(jnp.bfloat16)
    guess[...] = rounded
    wide = rounded.astype(jnp.float32)
    packed = []
    for part in range(mols // LANES):
        packed.append(wide[:LANES, part * LANES : (part + 1) * LANES].T)
    packed.append(jnp.concatenate([wide[LANES:, :LANES], wide[LANES:, LANES:]], axis=0).T)
    packed = jnp.concatenate(packed, axis=0).astype(jnp.bfloat16)
    for chip in range(rows.shape[0]):
        rows[chip] = packed


def rank_kernel(
    teams, domains, mols, info, near, dest, first_rows, rest_rows, half, wanted, label,
    ones, sums, named, ranks, known, spots,
):
    my_domain = info[0]
    listed = near[...]
    owner = listed // mols
    slot = listed % mols
    team = relative(owner % teams, info[3])
    offset = (owner // teams - my_domain + 1 + domains) % domains
    inside = offset == 1
    held_rows = mols * FEAT // LANES
    beyond = teams * held_rows + (offset // 2 * teams + team) * PACKED
    key = team * KEYS + offset
    keys = teams * KEYS
    square = (LANES, 2 * LANES)
    before = ((iota(square, 0) < iota(square, 1)) | (iota(square, 1) >= LANES)).astype(jnp.bfloat16)
    which = iota((keys, LANES), 0)
    who = iota((teams, LANES), 0)
    count = keys + teams
    blocks = listed.shape[0]
    for block in range(blocks):
        at = slice(block, block + 1)
        both = [jnp.where(which == key[at], 1.0, 0.0), jnp.where(who == team[at], 1.0, 0.0)]
        ones[block * count : (block + 1) * count, :] = jnp.concatenate(both, axis=0).astype(
            jnp.bfloat16
        )
    sums[...] = jnp.dot(ones[...], before, preferred_element_type=jnp.float32)
    carry = jnp.zeros((count, LANES), jnp.float32)
    last = jnp.zeros((1, LANES), jnp.int32)
    for block in range(blocks):
        at = slice(block, block + 1)
        cut = slice(block * LANES, (block + 1) * LANES)
        hit = which == key[at]
        peer = who == team[at]
        first = block * count
        prior = sums[first : first + count, :LANES] + carry
        carry = carry + sums[first : first + count, LANES:]
        rank = jnp.sum(jnp.where(hit, prior[:keys], 0.0), axis=0, keepdims=True).astype(jnp.int32)
        spot = jnp.sum(jnp.where(peer, prior[keys:], 0.0), axis=0, keepdims=True).astype(jnp.int32)
        last = jnp.maximum(last, spot)
        dest[at, :] = team[at] * WIDTH + spot
        base = team[at] * held_rows
        first_rows[at, :] = jnp.where(inside[at], base + slot[at], beyond[at] + rank)
        rest_rows[at, :] = jnp.where(
            inside[at],
            base + mols + slot[at] % LANES,
            beyond[at] + CAP + rank % (CAP // 2),
        )
        half[at, :] = jnp.where(inside[at], slot[at] // LANES, rank // (CAP // 2))
        name = slot[at].astype(jnp.float32)
        named[:, cut] = jnp.where(hit, name, 0.0).astype(jnp.bfloat16)
        ranks[:, cut] = (iota((LANES, LANES), 0) == rank).astype(jnp.bfloat16)
        side = offset[at].astype(jnp.float32)
        both = [jnp.where(peer, name, 0.0), jnp.where(peer, side, 0.0)]
        known[:, cut] = jnp.concatenate(both, axis=0).astype(jnp.bfloat16)
        spots[:, cut] = (iota((2 * LANES, LANES), 0) == spot).astype(jnp.bfloat16)
    names = lax.dot_general(named[...], ranks[...], NT, preferred_element_type=jnp.float32)
    filed = lax.dot_general(known[...], spots[...], NT, preferred_element_type=jnp.float32)
    wanted[...] = names.astype(jnp.int32)
    shift = info[3] % TAILS * SPARE
    back = (shift + LANES - SPARE) % LANES
    for at in range(2):
        part = filed[at * teams : (at + 1) * teams]
        label[2 * at] = part[:, :LANES]
        label[2 * at + 1] = pltpu.roll(part[:, LANES:], shift, 1)
        label[5 + at] = pltpu.roll(part[:, LANES:], back, 1)
    over = jnp.max(last, axis=1, keepdims=True) >= MAIN
    label[4] = jnp.broadcast_to(jnp.where(over, 1.0, 0.0), (teams, LANES))


def answer_kernel(from_lower, from_upper, same, other, to_lower, to_upper):
    count, held_rows = same.shape[:2]
    teams = 2 * count
    mols = held_rows * LANES // FEAT
    half = CAP // 2
    names = []
    for asked in (from_lower, from_upper):
        names.append(asked[...].astype(jnp.float32).T)
    low = iota((LANES, LANES), 1) < FEAT - LANES
    mol = iota((CAP, mols), 1).astype(jnp.float32)
    for team in range(teams):
        held, at = (same, team) if team < count else (other, team - count)
        packed = held[at, mols:, :].astype(jnp.float32)
        turned = pltpu.roll(packed, FEAT - LANES, 1)
        rest = jnp.concatenate([jnp.where(low, packed, turned), jnp.where(low, turned, packed)], axis=0)
        values = jnp.concatenate([held[at, :mols, :], rest.astype(jnp.bfloat16)], axis=1)
        hits = []
        for side in range(2):
            column = team * KEYS + 2 - 2 * side
            name = names[side][:CAP, column : column + 1]
            hits.append((name == mol).astype(jnp.bfloat16))
        found = jnp.dot(jnp.concatenate(hits, axis=0), values, preferred_element_type=jnp.float32)
        for side, out in enumerate((to_lower, to_upper)):
            mine = found[side * CAP : (side + 1) * CAP]
            out[team, :CAP, :] = mine[:, :LANES].astype(jnp.bfloat16)
            pair = jnp.where(low[:half], mine[:half, LANES:], mine[half:, LANES:])
            out[team, CAP:, :] = pair.astype(jnp.bfloat16)


def owners(mols, first, per_mol, count):
    mol = (iota((1, BLOCK), 1) + first) // per_mol
    mol = jnp.where(mol < count, mol, -1)
    return (iota((mols, BLOCK), 0) == mol).astype(jnp.bfloat16)


def turned_kernel(per_mol, dest, info, guess, blocks, label, out, spare, mine, turned, slots, stage, rest, sems):
    step = pl.program_id(0)
    teams = out.shape[0]
    width = WIDTH

    @pl.when(step == 0)
    def _():
        turned[...] = jnp.zeros_like(turned)

        def clear(team, _):
            start = pl.multiple_of(team * width, width)
            for part in range(3):
                slots[part, pl.ds(start, width), :] = jnp.zeros((width, LANES), jnp.float32)
            return 0

        lax.fori_loop(0, teams, clear, 0)

    table = owners(guess.shape[1], step * BLOCK, per_mol, info[1])
    mine[...] = jnp.dot(guess[...], table, preferred_element_type=jnp.float32)

    def move(line):
        for first in range(0, LANES, MOVES):
            places = [dest[line + first + i] for i in range(MOVES)]
            rows = [
                [turned[part, first + i : first + i + 1, :] for part in range(3)]
                for i in range(MOVES)
            ]
            for place, row in zip(places, rows):
                for part in range(3):
                    slots[part, pl.ds(place, 1), :] = row[part]

    def column(at, _):
        cut = pl.ds(pl.multiple_of(at * LANES, LANES), LANES)
        move(jnp.maximum(step * BLOCK + (at - 1) * LANES, 0))
        results = []
        for side in range(2):
            sums = [[None] * 3 for _ in range(OCC)]
            for inner in range(BAS):
                first = (side * BAS + inner) * BAS
                block = [
                    blocks[first + 8 * g : first + 8 * g + 8, cut].astype(jnp.float32) for g in range(3)
                ]
                for k in range(OCC):
                    row = mine[inner * OCC + k : inner * OCC + k + 1, cut]
                    for g in range(3):
                        term = block[g] * row
                        sums[k][g] = term if inner == 0 else sums[k][g] + term
            results += [sums[k][g] for k in range(OCC) for g in range(3)]
        for part in range(3):
            turned[part] = jnp.concatenate(results[part * 16 : part * 16 + 16], axis=0).T

        return 0

    lax.fori_loop(0, BLOCK // LANES, column, 0)

    @pl.when(step == pl.num_programs(0) - 1)
    def _():
        move((step + 1) * BLOCK - LANES)

        def copies(team):
            peer = absolute(team, info[3])
            return [
                pltpu.make_async_copy(stage.at[team], out.at[peer], sems.at[0, team]),
                pltpu.make_async_copy(rest.at[team], spare.at[peer], sems.at[1, team]),
            ]

        def finish(team, _):
            start = pl.multiple_of(team * width, width)
            for part in range(3):
                stage[team, part * MAIN : (part + 1) * MAIN, :] = slots[
                    part, pl.ds(start, MAIN), :
                ].astype(jnp.bfloat16)
                rest[team, part * SPARE : (part + 1) * SPARE, :] = slots[
                    part, pl.ds(start + MAIN, SPARE), :
                ].astype(jnp.bfloat16)
            names = [label[row, pl.ds(team, 1), :] for row in range(7)]
            fill = jnp.zeros((16, LANES), jnp.float32)
            stage[team, 3 * MAIN :, :] = jnp.concatenate(names[:5] + [fill[5:]], axis=0).astype(
                jnp.bfloat16
            )
            rest[team, 3 * SPARE :, :] = jnp.concatenate(names[5:] + [fill[2:]], axis=0).astype(
                jnp.bfloat16
            )
            for copy in copies(team):
                copy.start()
            return 0

        def wait(team, _):
            for copy in copies(team):
                copy.wait()
            return 0

        lax.fori_loop(0, teams, finish, 0)
        lax.fori_loop(0, teams, wait, 0)


def apply_blocks(wide, theirs, applied, mine, cut):
    other = [theirs[OCC * b : OCC * b + OCC, :] for b in range(BAS)]
    reduced = [[None] * OCC for _ in range(2)]
    for a in range(BAS):
        for side in range(2):
            first = (side * BAS + a) * BAS
            total = None
            for b in range(BAS):
                term = wide[first + b : first + b + 1, :] * other[b]
                total = term if total is None else total + term
            row = (side * BAS + a) * OCC
            applied[row : row + OCC, cut] = total
            if mine is not None:
                for k in range(OCC):
                    term = mine[a * OCC + k : a * OCC + k + 1, cut] * total
                    reduced[side][k] = term if a == 0 else reduced[side][k] + term
    return reduced


def diagonal_kernel(guess, blocks, out, wide, mine):
    wide[...] = blocks[...].astype(jnp.float32)
    mine[...] = guess[...].astype(jnp.float32)
    apply_blocks(wide, mine, out, None, slice(0, LANES))


def pairs_kernel(
    per_mol, first_rows, rest_rows, info, guess, blocks, half, local, same, other, lower, upper, scores, total,
    wide, mine, theirs, applied, near_a, near_b, held,
):
    step = pl.program_id(0)
    mols = guess.shape[1]

    @pl.when(step == 0)
    def _():
        total[...] = local[...]

        base = 0
        for source in (same, other, lower, upper):
            rows = source.shape[1]

            def widen(team, _):
                start = pl.multiple_of(base + team * rows, rows)
                held[pl.ds(start, rows), :] = source[team].astype(jnp.float32)
                return 0

            lax.fori_loop(0, source.shape[0], widen, 0)
            base += source.shape[0] * rows

    table = owners(mols, step * BLOCK, per_mol, info[1])
    mine[...] = jnp.dot(guess[...], table, preferred_element_type=jnp.float32)

    def pick(line):
        for first in range(0, LANES, MOVES):
            for index, near in ((first_rows, near_a), (rest_rows, near_b)):
                places = [index[line * LANES + first + i] for i in range(MOVES)]
                rows = [held[pl.ds(place, 1), :] for place in places]
                near[first : first + MOVES, :] = jnp.concatenate(rows, axis=0)

    @pl.when(step == 0)
    def _():
        pick(0)

    def column(at, _):
        cut = pl.ds(pl.multiple_of(at * LANES, LANES), LANES)
        line = step * (BLOCK // LANES) + at
        theirs[:LANES, :] = near_a[...].T
        rest = near_b[...].T
        theirs[LANES:, :] = jnp.where(
            half[pl.ds(line, 1), :] > 0, rest[FEAT - LANES :], rest[: FEAT - LANES]
        )
        pick(jnp.minimum(line + 1, half.shape[0] - 1))
        wide[...] = blocks[:, cut].astype(jnp.float32)
        reduced = apply_blocks(wide, theirs, applied, mine, cut)
        scores[:, cut] = jnp.concatenate(reduced[0] + reduced[1], axis=0)
        return 0

    lax.fori_loop(0, BLOCK // LANES, column, 0)
    total[...] += lax.dot_general(
        applied[...].astype(jnp.bfloat16), table, NT, preferred_element_type=jnp.float32
    )


def tail_names(labels, low, high, mols):
    lane = iota((1, LANES), 1) // SPARE
    names = jnp.zeros((1, LANES), jnp.float32)
    for at, label in enumerate(labels):
        name = label[low : low + 1] + label[high : high + 1] * mols
        names = jnp.where(lane == at, name, names)
    return names


def collect_kernel(blocks, lower, here, upper, over, sums, flags):
    step = pl.program_id(0)
    mols = here.shape[0]

    @pl.when(step == 0)
    def _():
        sums[...] = jnp.zeros_like(sums)
        flags[...] = jnp.zeros_like(flags)

    peers = range(blocks.shape[0])
    labels = [blocks[i, 3 * MAIN :, :].astype(jnp.float32) for i in peers]
    names = [label[0:1] + label[2:3] * mols for label in labels]
    for first in range(0, len(labels), TAILS):
        names.append(tail_names(labels[first : first + TAILS], 1, 3, mols))
    names = jnp.concatenate(names, axis=1)
    mol = iota((SIDES * mols, names.shape[1]), 0).astype(jnp.float32)
    values = []
    for part in range(3):
        row = part * MAIN
        rows = [blocks[i, row : row + LANES, :] for i in peers]
        rows += [blocks[i, row + LANES : row + MAIN, :] for i in peers]
        values.append(jnp.concatenate(rows, axis=0))
    sums[...] += jnp.dot(
        (mol == names).astype(jnp.bfloat16),
        jnp.concatenate(values, axis=1),
        preferred_element_type=jnp.float32,
    )
    for label in labels:
        flags[...] = jnp.maximum(flags[...], label[:8])

    @pl.when(step == pl.num_programs(0) - 1)
    def _():
        for side, out in enumerate((lower, here, upper)):
            out[...] = sums[side * mols : (side + 1) * mols].astype(out.dtype)
        over[0] = (jnp.max(flags[4:5, :]) > 0).astype(jnp.int32)


def spare_kernel(blocks, lower, here, upper, lower_out, here_out, upper_out):
    mols = here.shape[0]
    teams = blocks.shape[0]
    names = []
    for first in range(0, teams, TAILS):
        labels = [
            blocks[i, 3 * SPARE :, :].astype(jnp.float32) for i in range(first, first + TAILS)
        ]
        names.append(tail_names(labels, 0, 1, mols))
    mol = iota((SIDES * mols, teams * SPARE), 0).astype(jnp.float32)
    values = []
    for part in range(3):
        row = part * SPARE
        values.append(
            jnp.concatenate([blocks[i, row : row + SPARE, :] for i in range(teams)], axis=0)
        )
    sums = jnp.dot(
        (mol == jnp.concatenate(names, axis=1)).astype(jnp.bfloat16),
        jnp.concatenate(values, axis=1),
        preferred_element_type=jnp.float32,
    )
    pairs = ((lower, lower_out), (here, here_out), (upper, upper_out))
    for side, (before, out) in enumerate(pairs):
        part = sums[side * mols : (side + 1) * mols]
        out[...] = (before[...].astype(jnp.float32) + part).astype(out.dtype)


def finish_kernel(info, total, here, from_lower, from_upper, out):
    mols = here.shape[0]
    back = here[...] + from_lower[...].astype(jnp.float32) + from_upper[...].astype(jnp.float32)
    high = back.astype(jnp.bfloat16)
    low = (back - high.astype(jnp.float32)).astype(jnp.bfloat16)
    row = iota((ROWS, ROWS), 0)
    column = iota((ROWS, ROWS), 1)
    turn = (column // FEAT) * FEAT + column % BAS * OCC + column % FEAT // BAS
    order = (row == turn).astype(jnp.bfloat16)
    returned = lax.dot_general(order, high, NT, preferred_element_type=jnp.float32)
    returned = returned + lax.dot_general(order, low, NT, preferred_element_type=jnp.float32)
    alive = iota((ROWS, mols), 1) < info[1]
    out[...] = jnp.where(alive, total[...] + returned, 0.0)


def shifted(block, axis, distance):
    devices = range(lax.axis_size(axis))
    route = [((i - distance) % len(devices), i) for i in devices]
    return lax.ppermute(block, axis, route)


def params(mib=48):
    return pltpu.CompilerParams(vmem_limit_bytes=mib * 1024 * 1024)


def cost(us):
    return pl.CostEstimate(flops=0, transcendentals=0, bytes_accessed=us * 3_600_000)


def on_device(history, diag_blocks, pair_blocks, neighbours, counts):
    mols = history.shape[2]
    pairs = pair_blocks.shape[1]
    per_mol = pairs // mols
    teams = lax.axis_size("sub")
    domains = lax.axis_size("dom")
    columns = pairs // LANES
    held_rows = mols * FEAT // LANES
    shape = jax.ShapeDtypeStruct
    f32, bf16, i32 = jnp.float32, jnp.bfloat16, jnp.int32
    info = jnp.stack([lax.axis_index("dom"), counts[0], lax.axis_index("sub") % 2, lax.axis_index("sub")]).astype(i32)
    guess, rows = pl.pallas_call(
        predict_kernel,
        out_shape=(shape((FEAT, mols), bf16), shape((CHIPS, held_rows, LANES), bf16)),
        in_specs=[VMEM],
        out_specs=(VMEM,) * 2,
        compiler_params=params(),
        name="predict",
    )(history)

    table = shape((columns, LANES), i32)
    dest, first_rows, rest_rows, half, wanted, label = pl.pallas_call(
        functools.partial(rank_kernel, teams, domains, mols),
        out_shape=(table,) * 4 + (shape((teams * KEYS, LANES), i32), shape((7, teams, LANES), f32)),
        in_specs=[SMEM, VMEM],
        out_specs=(VMEM,) * 6,
        scratch_shapes=[
            pltpu.VMEM((columns * teams * (KEYS + 1), LANES), bf16),
            pltpu.VMEM((columns * teams * (KEYS + 1), 2 * LANES), f32),
            pltpu.VMEM((teams * KEYS, pairs), bf16),
            pltpu.VMEM((LANES, pairs), bf16),
            pltpu.VMEM((2 * teams, pairs), bf16),
            pltpu.VMEM((2 * LANES, pairs), bf16),
        ],
        compiler_params=params(),
        cost_estimate=cost(3),
        name="rank",
    )(info, neighbours.reshape(columns, LANES))
    dest, first_rows, rest_rows = (x.reshape(pairs) for x in (dest, first_rows, rest_rows))

    cores = [[2 * chip + core for chip in range(CHIPS)] for core in range(2)]
    same = lax.all_to_all(rows, "sub", 0, 0, tiled=True, axis_index_groups=cores)
    asked_lower, asked_upper = shifted(wanted, "dom", 1), shifted(wanted, "dom", -1)

    payload, spare = pl.pallas_call(
        functools.partial(turned_kernel, per_mol),
        grid=(pairs // BLOCK,),
        out_shape=(
            shape((teams, 3 * MAIN + 16, LANES), bf16),
            shape((teams, 3 * SPARE + 16, LANES), bf16),
        ),
        in_specs=[
            SMEM,
            SMEM,
            pl.BlockSpec((FEAT, mols), lambda i: (0, 0)),
            pl.BlockSpec((6 * FEAT, BLOCK), lambda i: (0, i)),
            pl.BlockSpec((7, teams, LANES), lambda i: (0, 0, 0)),
        ],
        out_specs=(pl.BlockSpec(memory_space=pltpu.HBM),) * 2,
        scratch_shapes=[
            pltpu.VMEM((FEAT, BLOCK), f32),
            pltpu.VMEM((3, LANES, LANES), f32),
            pltpu.VMEM((3, teams * WIDTH, LANES), f32),
            pltpu.VMEM((teams, 3 * MAIN + 16, LANES), bf16),
            pltpu.VMEM((teams, 3 * SPARE + 16, LANES), bf16),
            pltpu.SemaphoreType.DMA((2, teams)),
        ],
        compiler_params=params(60),
        cost_estimate=cost(25),
        name="turned",
    )(dest, info, guess, pair_blocks, label)

    payload, same, asked_lower, asked_upper = lax.optimization_barrier(
        (payload, same, asked_lower, asked_upper)
    )
    received = lax.all_to_all(payload, "sub", 0, 0, tiled=True)

    other = lax.ppermute(same, "sub", [(i ^ 1, i) for i in range(teams)])
    to_lower, to_upper = pl.pallas_call(
        answer_kernel,
        out_shape=(shape((teams, PACKED, LANES), bf16),) * 2,
        in_specs=[VMEM] * 4,
        out_specs=(VMEM,) * 2,
        compiler_params=params(),
        name="answer",
    )(asked_lower, asked_upper, same, other)
    upper = shifted(to_lower, "dom", -1)
    lower = shifted(to_upper, "dom", 1)

    local = pl.pallas_call(
        diagonal_kernel,
        grid=(mols // LANES,),
        out_shape=shape((ROWS, mols), f32),
        in_specs=[
            pl.BlockSpec((FEAT, LANES), lambda i: (0, i)),
            pl.BlockSpec((6 * FEAT, LANES), lambda i: (0, i)),
        ],
        out_specs=pl.BlockSpec((ROWS, LANES), lambda i: (0, i)),
        scratch_shapes=[
            pltpu.VMEM((6 * FEAT, LANES), f32),
            pltpu.VMEM((FEAT, LANES), f32),
        ],
        compiler_params=params(),
        name="diagonal",
    )(guess, diag_blocks)

    scores, total = pl.pallas_call(
        functools.partial(pairs_kernel, per_mol),
        grid=(pairs // BLOCK,),
        out_shape=(shape((ROWS // 3, pairs), f32), shape((ROWS, mols), f32)),
        in_specs=[
            SMEM,
            SMEM,
            SMEM,
            pl.BlockSpec((FEAT, mols), lambda i: (0, 0)),
            pl.BlockSpec((6 * FEAT, BLOCK), lambda i: (0, i)),
            pl.BlockSpec((columns, LANES), lambda i: (0, 0)),
            pl.BlockSpec((ROWS, mols), lambda i: (0, 0)),
            pl.BlockSpec((teams // 2, held_rows, LANES), lambda i: (0, 0, 0)),
            pl.BlockSpec((teams // 2, held_rows, LANES), lambda i: (0, 0, 0)),
            pl.BlockSpec((teams, PACKED, LANES), lambda i: (0, 0, 0)),
            pl.BlockSpec((teams, PACKED, LANES), lambda i: (0, 0, 0)),
        ],
        out_specs=(
            pl.BlockSpec((ROWS // 3, BLOCK), lambda i: (0, i)),
            pl.BlockSpec((ROWS, mols), lambda i: (0, 0)),
        ),
        scratch_shapes=[
            pltpu.VMEM((6 * FEAT, LANES), f32),
            pltpu.VMEM((FEAT, BLOCK), f32),
            pltpu.VMEM((FEAT, LANES), f32),
            pltpu.VMEM((ROWS, BLOCK), f32),
            pltpu.VMEM((LANES, LANES), f32),
            pltpu.VMEM((LANES, LANES), f32),
            pltpu.VMEM((teams * (held_rows + 2 * PACKED), LANES), f32),
        ],
        compiler_params=params(),
        cost_estimate=cost(35),
        name="pairs",
    )(first_rows, rest_rows, info, guess, pair_blocks, half, local, same, other, lower, upper)

    received, total = lax.optimization_barrier((received, total))
    whole = pl.BlockSpec((mols, ROWS), lambda i: (0, 0))
    group = 8
    sums_shape = (shape((mols, ROWS), bf16), shape((mols, ROWS), f32), shape((mols, ROWS), bf16))
    below, here, above, over = pl.pallas_call(
        collect_kernel,
        grid=(teams // group,),
        out_shape=sums_shape + (shape((1,), i32),),
        in_specs=[pl.BlockSpec((group, 3 * MAIN + 16, LANES), lambda i: (i, 0, 0))],
        out_specs=(whole,) * 3 + (SMEM,),
        scratch_shapes=[pltpu.VMEM((SIDES * mols, ROWS), f32), pltpu.VMEM((8, LANES), f32)],
        compiler_params=params(),
        name="collect",
    )(received)

    def second_round(spare, *sums):
        rest = lax.all_to_all(spare, "sub", 0, 0, tiled=True)
        return pl.pallas_call(
            spare_kernel,
            out_shape=sums_shape,
            in_specs=[VMEM] * 4,
            out_specs=(VMEM,) * 3,
            compiler_params=params(),
            name="spare",
        )(rest, *sums)

    below, here, above = lax.cond(
        over[0] > 0, second_round, lambda spare, *sums: sums, spare, below, here, above
    )
    from_lower, from_upper = shifted(above, "dom", 1), shifted(below, "dom", -1)

    products = pl.pallas_call(
        finish_kernel,
        out_shape=shape((ROWS, mols), f32),
        in_specs=[SMEM] + [VMEM] * 4,
        out_specs=VMEM,
        compiler_params=params(),
        name="finish",
    )(info, total, here, from_lower, from_upper)
    return products, scores


def solution(mesh):
    in_specs = (
        P(None, None, ("dom", "sub")),
        P(None, ("dom", "sub")),
        P(None, ("dom", "sub")),
        P(("dom", "sub")),
        P(("dom", "sub")),
    )
    out_specs = (P(None, ("dom", "sub")), P(None, ("dom", "sub")))
    return jax.shard_map(
        on_device, mesh=mesh, in_specs=in_specs, out_specs=out_specs, check_vma=False
    )
```

```python
import functools

import jax
import jax.numpy as jnp
from jax import lax
from jax.experimental import pallas as pl
from jax.experimental.pallas import tpu as pltpu
from jax.sharding import PartitionSpec as P

BAS = 24
OCC = 8
FEAT = BAS * OCC
ROWS = 2 * FEAT
CAP = 64
LANES = 128
BLOCK = 4 * LANES
MOVES = 16
SIDES = 3
CHIPS = 16
MAIN = 160
SPARE = SIDES * CAP - MAIN
TAILS = LANES // SPARE
KEYS = 4
ASPC_WEIGHTS = (2.8, -2.8, 1.2, -0.2)
VMEM = pl.BlockSpec(memory_space=pltpu.VMEM)
SMEM = pl.BlockSpec(memory_space=pltpu.SMEM)
NT = (((1,), (1,)), ((), ()))
WIDTH = SIDES * CAP
PACKED = CAP * FEAT // LANES


def iota(shape, dim):
    return lax.broadcasted_iota(jnp.int32, shape, dim)


def relative(team, me):
    return (team + me) % 2 * CHIPS + team // 2


def absolute(place, me):
    return place % CHIPS * 2 + (place // CHIPS + me) % 2


def predict_kernel(history, guess, rows):
    mols = guess.shape[1]
    total = ASPC_WEIGHTS[0] * history[0]
    for level in range(1, 4):
        total = total + ASPC_WEIGHTS[level] * history[level]
    rounded = total.astype(jnp.bfloat16)
    guess[...] = rounded
    wide = rounded.astype(jnp.float32)
    packed = []
    for part in range(mols // LANES):
        packed.append(wide[:LANES, part * LANES : (part + 1) * LANES].T)
    packed.append(jnp.concatenate([wide[LANES:, :LANES], wide[LANES:, LANES:]], axis=0).T)
    packed = jnp.concatenate(packed, axis=0).astype(jnp.bfloat16)
    for chip in range(rows.shape[0]):
        rows[chip] = packed


def rank_kernel(
    teams, domains, mols, info, near, dest, first_rows, rest_rows, half, wanted, label,
    ones, sums, named, ranks, known, spots,
):
    my_domain = info[0]
    listed = near[...]
    owner = listed // mols
    slot = listed % mols
    team = relative(owner % teams, info[3])
    offset = (owner // teams - my_domain + 1 + domains) % domains
    inside = offset == 1
    held_rows = mols * FEAT // LANES
    beyond = teams * held_rows + (offset // 2 * teams + team) * PACKED
    key = team * KEYS + offset
    keys = teams * KEYS
    square = (LANES, 2 * LANES)
    before = ((iota(square, 0) < iota(square, 1)) | (iota(square, 1) >= LANES)).astype(jnp.bfloat16)
    which = iota((keys, LANES), 0)
    who = iota((teams, LANES), 0)
    count = keys + teams
    blocks = listed.shape[0]
    for block in range(blocks):
        at = slice(block, block + 1)
        both = [jnp.where(which == key[at], 1.0, 0.0), jnp.where(who == team[at], 1.0, 0.0)]
        ones[block * count : (block + 1) * count, :] = jnp.concatenate(both, axis=0).astype(
            jnp.bfloat16
        )
    sums[...] = jnp.dot(ones[...], before, preferred_element_type=jnp.float32)
    carry = jnp.zeros((count, LANES), jnp.float32)
    last = jnp.zeros((1, LANES), jnp.int32)
    for block in range(blocks):
        at = slice(block, block + 1)
        cut = slice(block * LANES, (block + 1) * LANES)
        hit = which == key[at]
        peer = who == team[at]
        first = block * count
        prior = sums[first : first + count, :LANES] + carry
        carry = carry + sums[first : first + count, LANES:]
        rank = jnp.sum(jnp.where(hit, prior[:keys], 0.0), axis=0, keepdims=True).astype(jnp.int32)
        spot = jnp.sum(jnp.where(peer, prior[keys:], 0.0), axis=0, keepdims=True).astype(jnp.int32)
        last = jnp.maximum(last, spot)
        dest[at, :] = team[at] * WIDTH + spot
        base = team[at] * held_rows
        first_rows[at, :] = jnp.where(inside[at], base + slot[at], beyond[at] + rank)
        rest_rows[at, :] = jnp.where(
            inside[at],
            base + mols + slot[at] % LANES,
            beyond[at] + CAP + rank % (CAP // 2),
        )
        half[at, :] = jnp.where(inside[at], slot[at] // LANES, rank // (CAP // 2))
        name = slot[at].astype(jnp.float32)
        named[:, cut] = jnp.where(hit, name, 0.0).astype(jnp.bfloat16)
        ranks[:, cut] = (iota((LANES, LANES), 0) == rank).astype(jnp.bfloat16)
        side = offset[at].astype(jnp.float32)
        both = [jnp.where(peer, name, 0.0), jnp.where(peer, side, 0.0)]
        known[:, cut] = jnp.concatenate(both, axis=0).astype(jnp.bfloat16)
        spots[:, cut] = (iota((2 * LANES, LANES), 0) == spot).astype(jnp.bfloat16)
    names = lax.dot_general(named[...], ranks[...], NT, preferred_element_type=jnp.float32)
    filed = lax.dot_general(known[...], spots[...], NT, preferred_element_type=jnp.float32)
    wanted[...] = names.astype(jnp.int32)
    shift = info[3] % TAILS * SPARE
    back = (shift + LANES - SPARE) % LANES
    for at in range(2):
        part = filed[at * teams : (at + 1) * teams]
        label[2 * at] = part[:, :LANES]
        label[2 * at + 1] = pltpu.roll(part[:, LANES:], shift, 1)
        label[5 + at] = pltpu.roll(part[:, LANES:], back, 1)
    over = jnp.max(last, axis=1, keepdims=True) >= MAIN
    label[4] = jnp.broadcast_to(jnp.where(over, 1.0, 0.0), (teams, LANES))


def answer_kernel(from_lower, from_upper, same, other, to_lower, to_upper):
    count, held_rows = same.shape[:2]
    teams = 2 * count
    mols = held_rows * LANES // FEAT
    half = CAP // 2
    names = []
    for asked in (from_lower, from_upper):
        names.append(asked[...].astype(jnp.float32).T)
    low = iota((LANES, LANES), 1) < FEAT - LANES
    mol = iota((CAP, mols), 1).astype(jnp.float32)
    for team in range(teams):
        held, at = (same, team) if team < count else (other, team - count)
        packed = held[at, mols:, :].astype(jnp.float32)
        turned = pltpu.roll(packed, FEAT - LANES, 1)
        rest = jnp.concatenate([jnp.where(low, packed, turned), jnp.where(low, turned, packed)], axis=0)
        values = jnp.concatenate([held[at, :mols, :], rest.astype(jnp.bfloat16)], axis=1)
        hits = []
        for side in range(2):
            column = team * KEYS + 2 - 2 * side
            name = names[side][:CAP, column : column + 1]
            hits.append((name == mol).astype(jnp.bfloat16))
        found = jnp.dot(jnp.concatenate(hits, axis=0), values, preferred_element_type=jnp.float32)
        for side, out in enumerate((to_lower, to_upper)):
            mine = found[side * CAP : (side + 1) * CAP]
            out[team, :CAP, :] = mine[:, :LANES].astype(jnp.bfloat16)
            pair = jnp.where(low[:half], mine[:half, LANES:], mine[half:, LANES:])
            out[team, CAP:, :] = pair.astype(jnp.bfloat16)


def owners(mols, first, per_mol, count):
    mol = (iota((1, BLOCK), 1) + first) // per_mol
    mol = jnp.where(mol < count, mol, -1)
    return (iota((mols, BLOCK), 0) == mol).astype(jnp.bfloat16)


def turned_kernel(per_mol, dest, info, guess, blocks, label, out, spare, mine, turned, slots, stage, rest, sems):
    step = pl.program_id(0)
    teams = out.shape[0]
    width = WIDTH

    @pl.when(step == 0)
    def _():
        turned[...] = jnp.zeros_like(turned)

        def clear(team, _):
            start = pl.multiple_of(team * width, width)
            for part in range(3):
                slots[part, pl.ds(start, width), :] = jnp.zeros((width, LANES), jnp.float32)
            return 0

        lax.fori_loop(0, teams, clear, 0)

    table = owners(guess.shape[1], step * BLOCK, per_mol, info[1])
    mine[...] = jnp.dot(guess[...], table, preferred_element_type=jnp.float32)

    def move(line):
        for first in range(0, LANES, MOVES):
            places = [dest[line + first + i] for i in range(MOVES)]
            rows = [
                [turned[part, first + i : first + i + 1, :] for part in range(3)]
                for i in range(MOVES)
            ]
            for place, row in zip(places, rows):
                for part in range(3):
                    slots[part, pl.ds(place, 1), :] = row[part]

    def column(at, _):
        cut = pl.ds(pl.multiple_of(at * LANES, LANES), LANES)
        move(jnp.maximum(step * BLOCK + (at - 1) * LANES, 0))
        results = []
        for side in range(2):
            sums = [[None] * 3 for _ in range(OCC)]
            for inner in range(BAS):
                first = (side * BAS + inner) * BAS
                block = [
                    blocks[first + 8 * g : first + 8 * g + 8, cut].astype(jnp.float32) for g in range(3)
                ]
                for k in range(OCC):
                    row = mine[inner * OCC + k : inner * OCC + k + 1, cut]
                    for g in range(3):
                        term = block[g] * row
                        sums[k][g] = term if inner == 0 else sums[k][g] + term
            results += [sums[k][g] for k in range(OCC) for g in range(3)]
        for part in range(3):
            turned[part] = jnp.concatenate(results[part * 16 : part * 16 + 16], axis=0).T

        return 0

    lax.fori_loop(0, BLOCK // LANES, column, 0)

    @pl.when(step == pl.num_programs(0) - 1)
    def _():
        move((step + 1) * BLOCK - LANES)

        def copies(team):
            peer = absolute(team, info[3])
            return [
                pltpu.make_async_copy(stage.at[team], out.at[peer], sems.at[0, team]),
                pltpu.make_async_copy(rest.at[team], spare.at[peer], sems.at[1, team]),
            ]

        def finish(team, _):
            start = pl.multiple_of(team * width, width)
            for part in range(3):
                stage[team, part * MAIN : (part + 1) * MAIN, :] = slots[
                    part, pl.ds(start, MAIN), :
                ].astype(jnp.bfloat16)
                rest[team, part * SPARE : (part + 1) * SPARE, :] = slots[
                    part, pl.ds(start + MAIN, SPARE), :
                ].astype(jnp.bfloat16)
            names = [label[row, pl.ds(team, 1), :] for row in range(7)]
            fill = jnp.zeros((16, LANES), jnp.float32)
            stage[team, 3 * MAIN :, :] = jnp.concatenate(names[:5] + [fill[5:]], axis=0).astype(
                jnp.bfloat16
            )
            rest[team, 3 * SPARE :, :] = jnp.concatenate(names[5:] + [fill[2:]], axis=0).astype(
                jnp.bfloat16
            )
            for copy in copies(team):
                copy.start()
            return 0

        def wait(team, _):
            for copy in copies(team):
                copy.wait()
            return 0

        lax.fori_loop(0, teams, finish, 0)
        lax.fori_loop(0, teams, wait, 0)


def apply_blocks(wide, theirs, applied, mine, cut):
    other = [theirs[OCC * b : OCC * b + OCC, :] for b in range(BAS)]
    reduced = [[None] * OCC for _ in range(2)]
    for a in range(BAS):
        for side in range(2):
            first = (side * BAS + a) * BAS
            total = None
            for b in range(BAS):
                term = wide[first + b : first + b + 1, :] * other[b]
                total = term if total is None else total + term
            row = (side * BAS + a) * OCC
            applied[row : row + OCC, cut] = total
            if mine is not None:
                for k in range(OCC):
                    term = mine[a * OCC + k : a * OCC + k + 1, cut] * total
                    reduced[side][k] = term if a == 0 else reduced[side][k] + term
    return reduced


def diagonal_kernel(guess, blocks, out, wide, mine):
    wide[...] = blocks[...].astype(jnp.float32)
    mine[...] = guess[...].astype(jnp.float32)
    apply_blocks(wide, mine, out, None, slice(0, LANES))


def pairs_kernel(
    per_mol, first_rows, rest_rows, info, guess, blocks, half, local, same, other, lower, upper, scores, total,
    wide, mine, theirs, applied, near_a, near_b, held,
):
    step = pl.program_id(0)
    mols = guess.shape[1]

    @pl.when(step == 0)
    def _():
        total[...] = local[...]

        base = 0
        for source in (same, other, lower, upper):
            rows = source.shape[1]

            def widen(team, _):
                start = pl.multiple_of(base + team * rows, rows)
                held[pl.ds(start, rows), :] = source[team].astype(jnp.float32)
                return 0

            lax.fori_loop(0, source.shape[0], widen, 0)
            base += source.shape[0] * rows

    table = owners(mols, step * BLOCK, per_mol, info[1])
    mine[...] = jnp.dot(guess[...], table, preferred_element_type=jnp.float32)

    def pick(line):
        for first in range(0, LANES, MOVES):
            for index, near in ((first_rows, near_a), (rest_rows, near_b)):
                places = [index[line * LANES + first + i] for i in range(MOVES)]
                rows = [held[pl.ds(place, 1), :] for place in places]
                near[first : first + MOVES, :] = jnp.concatenate(rows, axis=0)

    @pl.when(step == 0)
    def _():
        pick(0)

    def column(at, _):
        cut = pl.ds(pl.multiple_of(at * LANES, LANES), LANES)
        line = step * (BLOCK // LANES) + at
        theirs[:LANES, :] = near_a[...].T
        rest = near_b[...].T
        theirs[LANES:, :] = jnp.where(
            half[pl.ds(line, 1), :] > 0, rest[FEAT - LANES :], rest[: FEAT - LANES]
        )
        pick(jnp.minimum(line + 1, half.shape[0] - 1))
        wide[...] = blocks[:, cut].astype(jnp.float32)
        reduced = apply_blocks(wide, theirs, applied, mine, cut)
        scores[:, cut] = jnp.concatenate(reduced[0] + reduced[1], axis=0)
        return 0

    lax.fori_loop(0, BLOCK // LANES, column, 0)
    total[...] += lax.dot_general(
        applied[...].astype(jnp.bfloat16), table, NT, preferred_element_type=jnp.float32
    )


def tail_names(labels, low, high, mols):
    lane = iota((1, LANES), 1) // SPARE
    names = jnp.zeros((1, LANES), jnp.float32)
    for at, label in enumerate(labels):
        name = label[low : low + 1] + label[high : high + 1] * mols
        names = jnp.where(lane == at, name, names)
    return names


def collect_kernel(blocks, lower, here, upper, over, sums, flags):
    step = pl.program_id(0)
    mols = here.shape[0]

    @pl.when(step == 0)
    def _():
        sums[...] = jnp.zeros_like(sums)
        flags[...] = jnp.zeros_like(flags)

    peers = range(blocks.shape[0])
    labels = [blocks[i, 3 * MAIN :, :].astype(jnp.float32) for i in peers]
    names = [label[0:1] + label[2:3] * mols for label in labels]
    for first in range(0, len(labels), TAILS):
        names.append(tail_names(labels[first : first + TAILS], 1, 3, mols))
    names = jnp.concatenate(names, axis=1)
    mol = iota((SIDES * mols, names.shape[1]), 0).astype(jnp.float32)
    values = []
    for part in range(3):
        row = part * MAIN
        rows = [blocks[i, row : row + LANES, :] for i in peers]
        rows += [blocks[i, row + LANES : row + MAIN, :] for i in peers]
        values.append(jnp.concatenate(rows, axis=0))
    sums[...] += jnp.dot(
        (mol == names).astype(jnp.bfloat16),
        jnp.concatenate(values, axis=1),
        preferred_element_type=jnp.float32,
    )
    for label in labels:
        flags[...] = jnp.maximum(flags[...], label[:8])

    @pl.when(step == pl.num_programs(0) - 1)
    def _():
        for side, out in enumerate((lower, here, upper)):
            out[...] = sums[side * mols : (side + 1) * mols].astype(out.dtype)
        over[0] = (jnp.max(flags[4:5, :]) > 0).astype(jnp.int32)


def spare_kernel(blocks, lower, here, upper, lower_out, here_out, upper_out):
    mols = here.shape[0]
    teams = blocks.shape[0]
    names = []
    for first in range(0, teams, TAILS):
        labels = [
            blocks[i, 3 * SPARE :, :].astype(jnp.float32) for i in range(first, first + TAILS)
        ]
        names.append(tail_names(labels, 0, 1, mols))
    mol = iota((SIDES * mols, teams * SPARE), 0).astype(jnp.float32)
    values = []
    for part in range(3):
        row = part * SPARE
        values.append(
            jnp.concatenate([blocks[i, row : row + SPARE, :] for i in range(teams)], axis=0)
        )
    sums = jnp.dot(
        (mol == jnp.concatenate(names, axis=1)).astype(jnp.bfloat16),
        jnp.concatenate(values, axis=1),
        preferred_element_type=jnp.float32,
    )
    pairs = ((lower, lower_out), (here, here_out), (upper, upper_out))
    for side, (before, out) in enumerate(pairs):
        part = sums[side * mols : (side + 1) * mols]
        out[...] = (before[...].astype(jnp.float32) + part).astype(out.dtype)


def finish_kernel(info, total, here, from_lower, from_upper, out):
    mols = here.shape[0]
    back = here[...] + from_lower[...].astype(jnp.float32) + from_upper[...].astype(jnp.float32)
    high = back.astype(jnp.bfloat16)
    low = (back - high.astype(jnp.float32)).astype(jnp.bfloat16)
    row = iota((ROWS, ROWS), 0)
    column = iota((ROWS, ROWS), 1)
    turn = (column // FEAT) * FEAT + column % BAS * OCC + column % FEAT // BAS
    order = (row == turn).astype(jnp.bfloat16)
    returned = lax.dot_general(order, high, NT, preferred_element_type=jnp.float32)
    returned = returned + lax.dot_general(order, low, NT, preferred_element_type=jnp.float32)
    alive = iota((ROWS, mols), 1) < info[1]
    out[...] = jnp.where(alive, total[...] + returned, 0.0)


def shifted(block, axis, distance):
    devices = range(lax.axis_size(axis))
    route = [((i - distance) % len(devices), i) for i in devices]
    return lax.ppermute(block, axis, route)


def params(mib=48):
    return pltpu.CompilerParams(vmem_limit_bytes=mib * 1024 * 1024)


def cost(us):
    return pl.CostEstimate(flops=0, transcendentals=0, bytes_accessed=us * 3_600_000)


def on_device(history, diag_blocks, pair_blocks, neighbours, counts):
    mols = history.shape[2]
    pairs = pair_blocks.shape[1]
    per_mol = pairs // mols
    teams = lax.axis_size("sub")
    domains = lax.axis_size("dom")
    columns = pairs // LANES
    held_rows = mols * FEAT // LANES
    shape = jax.ShapeDtypeStruct
    f32, bf16, i32 = jnp.float32, jnp.bfloat16, jnp.int32
    info = jnp.stack([lax.axis_index("dom"), counts[0], lax.axis_index("sub") % 2, lax.axis_index("sub")]).astype(i32)
    guess, rows = pl.pallas_call(
        predict_kernel,
        out_shape=(shape((FEAT, mols), bf16), shape((CHIPS, held_rows, LANES), bf16)),
        in_specs=[VMEM],
        out_specs=(VMEM,) * 2,
        compiler_params=params(60),
        name="predict",
    )(history)

    table = shape((columns, LANES), i32)
    dest, first_rows, rest_rows, half, wanted, label = pl.pallas_call(
        functools.partial(rank_kernel, teams, domains, mols),
        out_shape=(table,) * 4 + (shape((teams * KEYS, LANES), i32), shape((7, teams, LANES), f32)),
        in_specs=[SMEM, VMEM],
        out_specs=(VMEM,) * 6,
        scratch_shapes=[
            pltpu.VMEM((columns * teams * (KEYS + 1), LANES), bf16),
            pltpu.VMEM((columns * teams * (KEYS + 1), 2 * LANES), f32),
            pltpu.VMEM((teams * KEYS, pairs), bf16),
            pltpu.VMEM((LANES, pairs), bf16),
            pltpu.VMEM((2 * teams, pairs), bf16),
            pltpu.VMEM((2 * LANES, pairs), bf16),
        ],
        compiler_params=params(),
        cost_estimate=cost(3),
        name="rank",
    )(info, neighbours.reshape(columns, LANES))
    dest, first_rows, rest_rows = (x.reshape(pairs) for x in (dest, first_rows, rest_rows))

    cores = [[2 * chip + core for chip in range(CHIPS)] for core in range(2)]
    same = lax.all_to_all(rows, "sub", 0, 0, tiled=True, axis_index_groups=cores)
    asked_lower, asked_upper = shifted(wanted, "dom", 1), shifted(wanted, "dom", -1)

    payload, spare = pl.pallas_call(
        functools.partial(turned_kernel, per_mol),
        grid=(pairs // BLOCK,),
        out_shape=(
            shape((teams, 3 * MAIN + 16, LANES), bf16),
            shape((teams, 3 * SPARE + 16, LANES), bf16),
        ),
        in_specs=[
            SMEM,
            SMEM,
            pl.BlockSpec((FEAT, mols), lambda i: (0, 0)),
            pl.BlockSpec((6 * FEAT, BLOCK), lambda i: (0, i)),
            pl.BlockSpec((7, teams, LANES), lambda i: (0, 0, 0)),
        ],
        out_specs=(pl.BlockSpec(memory_space=pltpu.HBM),) * 2,
        scratch_shapes=[
            pltpu.VMEM((FEAT, BLOCK), f32),
            pltpu.VMEM((3, LANES, LANES), f32),
            pltpu.VMEM((3, teams * WIDTH, LANES), f32),
            pltpu.VMEM((teams, 3 * MAIN + 16, LANES), bf16),
            pltpu.VMEM((teams, 3 * SPARE + 16, LANES), bf16),
            pltpu.SemaphoreType.DMA((2, teams)),
        ],
        compiler_params=params(60),
        cost_estimate=cost(25),
        name="turned",
    )(dest, info, guess, pair_blocks, label)

    payload, same, asked_lower, asked_upper = lax.optimization_barrier(
        (payload, same, asked_lower, asked_upper)
    )
    received = lax.all_to_all(payload, "sub", 0, 0, tiled=True)

    other = lax.ppermute(same, "sub", [(i ^ 1, i) for i in range(teams)])
    to_lower, to_upper = pl.pallas_call(
        answer_kernel,
        out_shape=(shape((teams, PACKED, LANES), bf16),) * 2,
        in_specs=[VMEM] * 4,
        out_specs=(VMEM,) * 2,
        compiler_params=params(),
        name="answer",
    )(asked_lower, asked_upper, same, other)
    upper = shifted(to_lower, "dom", -1)
    lower = shifted(to_upper, "dom", 1)

    local = pl.pallas_call(
        diagonal_kernel,
        grid=(mols // LANES,),
        out_shape=shape((ROWS, mols), f32),
        in_specs=[
            pl.BlockSpec((FEAT, LANES), lambda i: (0, i)),
            pl.BlockSpec((6 * FEAT, LANES), lambda i: (0, i)),
        ],
        out_specs=pl.BlockSpec((ROWS, LANES), lambda i: (0, i)),
        scratch_shapes=[
            pltpu.VMEM((6 * FEAT, LANES), f32),
            pltpu.VMEM((FEAT, LANES), f32),
        ],
        compiler_params=params(),
        name="diagonal",
    )(guess, diag_blocks)

    scores, total = pl.pallas_call(
        functools.partial(pairs_kernel, per_mol),
        grid=(pairs // BLOCK,),
        out_shape=(shape((ROWS // 3, pairs), f32), shape((ROWS, mols), f32)),
        in_specs=[
            SMEM,
            SMEM,
            SMEM,
            pl.BlockSpec((FEAT, mols), lambda i: (0, 0)),
            pl.BlockSpec((6 * FEAT, BLOCK), lambda i: (0, i)),
            pl.BlockSpec((columns, LANES), lambda i: (0, 0)),
            pl.BlockSpec((ROWS, mols), lambda i: (0, 0)),
            pl.BlockSpec((teams // 2, held_rows, LANES), lambda i: (0, 0, 0)),
            pl.BlockSpec((teams // 2, held_rows, LANES), lambda i: (0, 0, 0)),
            pl.BlockSpec((teams, PACKED, LANES), lambda i: (0, 0, 0)),
            pl.BlockSpec((teams, PACKED, LANES), lambda i: (0, 0, 0)),
        ],
        out_specs=(
            pl.BlockSpec((ROWS // 3, BLOCK), lambda i: (0, i)),
            pl.BlockSpec((ROWS, mols), lambda i: (0, 0)),
        ),
        scratch_shapes=[
            pltpu.VMEM((6 * FEAT, LANES), f32),
            pltpu.VMEM((FEAT, BLOCK), f32),
            pltpu.VMEM((FEAT, LANES), f32),
            pltpu.VMEM((ROWS, BLOCK), f32),
            pltpu.VMEM((LANES, LANES), f32),
            pltpu.VMEM((LANES, LANES), f32),
            pltpu.VMEM((teams * (held_rows + 2 * PACKED), LANES), f32),
        ],
        compiler_params=params(),
        cost_estimate=cost(35),
        name="pairs",
    )(first_rows, rest_rows, info, guess, pair_blocks, half, local, same, other, lower, upper)

    received, total = lax.optimization_barrier((received, total))
    whole = pl.BlockSpec((mols, ROWS), lambda i: (0, 0))
    group = 8
    sums_shape = (shape((mols, ROWS), bf16), shape((mols, ROWS), f32), shape((mols, ROWS), bf16))
    below, here, above, over = pl.pallas_call(
        collect_kernel,
        grid=(teams // group,),
        out_shape=sums_shape + (shape((1,), i32),),
        in_specs=[pl.BlockSpec((group, 3 * MAIN + 16, LANES), lambda i: (i, 0, 0))],
        out_specs=(whole,) * 3 + (SMEM,),
        scratch_shapes=[pltpu.VMEM((SIDES * mols, ROWS), f32), pltpu.VMEM((8, LANES), f32)],
        compiler_params=params(),
        name="collect",
    )(received)

    def second_round(spare, *sums):
        rest = lax.all_to_all(spare, "sub", 0, 0, tiled=True)
        return pl.pallas_call(
            spare_kernel,
            out_shape=sums_shape,
            in_specs=[VMEM] * 4,
            out_specs=(VMEM,) * 3,
            compiler_params=params(),
            name="spare",
        )(rest, *sums)

    below, here, above = lax.cond(
        over[0] > 0, second_round, lambda spare, *sums: sums, spare, below, here, above
    )
    from_lower, from_upper = shifted(above, "dom", 1), shifted(below, "dom", -1)

    products = pl.pallas_call(
        finish_kernel,
        out_shape=shape((ROWS, mols), f32),
        in_specs=[SMEM] + [VMEM] * 4,
        out_specs=VMEM,
        compiler_params=params(),
        name="finish",
    )(info, total, here, from_lower, from_upper)
    return products, scores


def solution(mesh):
    in_specs = (
        P(None, None, ("dom", "sub")),
        P(None, ("dom", "sub")),
        P(None, ("dom", "sub")),
        P(("dom", "sub")),
        P(("dom", "sub")),
    )
    out_specs = (P(None, ("dom", "sub")), P(None, ("dom", "sub")))
    return jax.shard_map(
        on_device, mesh=mesh, in_specs=in_specs, out_specs=out_specs, check_vma=False
    )
```

```python
import functools

import jax
import jax.numpy as jnp
from jax import lax
from jax.experimental import pallas as pl
from jax.experimental.pallas import tpu as pltpu
from jax.sharding import PartitionSpec as P

BAS = 24
OCC = 8
FEAT = BAS * OCC
ROWS = 2 * FEAT
CAP = 64
LANES = 128
BLOCK = 4 * LANES
MOVES = 16
SIDES = 3
CHIPS = 16
MAIN = 160
SPARE = SIDES * CAP - MAIN
TAILS = LANES // SPARE
KEYS = 4
ASPC_WEIGHTS = (2.8, -2.8, 1.2, -0.2)
VMEM = pl.BlockSpec(memory_space=pltpu.VMEM)
SMEM = pl.BlockSpec(memory_space=pltpu.SMEM)
NT = (((1,), (1,)), ((), ()))
WIDTH = SIDES * CAP
PACKED = CAP * FEAT // LANES


def iota(shape, dim):
    return lax.broadcasted_iota(jnp.int32, shape, dim)


def relative(team, me):
    return (team + me) % 2 * CHIPS + team // 2


def absolute(place, me):
    return place % CHIPS * 2 + (place // CHIPS + me) % 2


def predict_kernel(history, guess, rows):
    mols = guess.shape[1]
    total = ASPC_WEIGHTS[0] * history[0]
    for level in range(1, 4):
        total = total + ASPC_WEIGHTS[level] * history[level]
    rounded = total.astype(jnp.bfloat16)
    guess[...] = rounded
    wide = rounded.astype(jnp.float32)
    packed = []
    for part in range(mols // LANES):
        packed.append(wide[:LANES, part * LANES : (part + 1) * LANES].T)
    packed.append(jnp.concatenate([wide[LANES:, :LANES], wide[LANES:, LANES:]], axis=0).T)
    packed = jnp.concatenate(packed, axis=0).astype(jnp.bfloat16)
    for chip in range(rows.shape[0]):
        rows[chip] = packed


def rank_kernel(
    teams, domains, mols, info, near, dest, first_rows, rest_rows, half, wanted, label,
    ones, sums, named, ranks, known, spots,
):
    my_domain = info[0]
    listed = near[...]
    owner = listed // mols
    slot = listed % mols
    team = relative(owner % teams, info[3])
    offset = (owner // teams - my_domain + 1 + domains) % domains
    inside = offset == 1
    held_rows = mols * FEAT // LANES
    beyond = teams * held_rows + (offset // 2 * teams + team) * PACKED
    key = team * KEYS + offset
    keys = teams * KEYS
    square = (LANES, 2 * LANES)
    before = ((iota(square, 0) < iota(square, 1)) | (iota(square, 1) >= LANES)).astype(jnp.bfloat16)
    which = iota((keys, LANES), 0)
    who = iota((teams, LANES), 0)
    count = keys + teams
    blocks = listed.shape[0]
    for block in range(blocks):
        at = slice(block, block + 1)
        both = [jnp.where(which == key[at], 1.0, 0.0), jnp.where(who == team[at], 1.0, 0.0)]
        ones[block * count : (block + 1) * count, :] = jnp.concatenate(both, axis=0).astype(
            jnp.bfloat16
        )
    sums[...] = jnp.dot(ones[...], before, preferred_element_type=jnp.float32)
    carry = jnp.zeros((count, LANES), jnp.float32)
    last = jnp.zeros((1, LANES), jnp.int32)
    for block in range(blocks):
        at = slice(block, block + 1)
        cut = slice(block * LANES, (block + 1) * LANES)
        hit = which == key[at]
        peer = who == team[at]
        first = block * count
        prior = sums[first : first + count, :LANES] + carry
        carry = carry + sums[first : first + count, LANES:]
        rank = jnp.sum(jnp.where(hit, prior[:keys], 0.0), axis=0, keepdims=True).astype(jnp.int32)
        spot = jnp.sum(jnp.where(peer, prior[keys:], 0.0), axis=0, keepdims=True).astype(jnp.int32)
        last = jnp.maximum(last, spot)
        dest[at, :] = team[at] * WIDTH + spot
        base = team[at] * held_rows
        first_rows[at, :] = jnp.where(inside[at], base + slot[at], beyond[at] + rank)
        rest_rows[at, :] = jnp.where(
            inside[at],
            base + mols + slot[at] % LANES,
            beyond[at] + CAP + rank % (CAP // 2),
        )
        half[at, :] = jnp.where(inside[at], slot[at] // LANES, rank // (CAP // 2))
        name = slot[at].astype(jnp.float32)
        named[:, cut] = jnp.where(hit, name, 0.0).astype(jnp.bfloat16)
        ranks[:, cut] = (iota((LANES, LANES), 0) == rank).astype(jnp.bfloat16)
        side = offset[at].astype(jnp.float32)
        both = [jnp.where(peer, name, 0.0), jnp.where(peer, side, 0.0)]
        known[:, cut] = jnp.concatenate(both, axis=0).astype(jnp.bfloat16)
        spots[:, cut] = (iota((2 * LANES, LANES), 0) == spot).astype(jnp.bfloat16)
    names = lax.dot_general(named[...], ranks[...], NT, preferred_element_type=jnp.float32)
    filed = lax.dot_general(known[...], spots[...], NT, preferred_element_type=jnp.float32)
    wanted[...] = names.astype(jnp.int32)
    shift = info[3] % TAILS * SPARE
    back = (shift + LANES - SPARE) % LANES
    for at in range(2):
        part = filed[at * teams : (at + 1) * teams]
        label[2 * at] = part[:, :LANES]
        label[2 * at + 1] = pltpu.roll(part[:, LANES:], shift, 1)
        label[5 + at] = pltpu.roll(part[:, LANES:], back, 1)
    over = jnp.max(last, axis=1, keepdims=True) >= MAIN
    label[4] = jnp.broadcast_to(jnp.where(over, 1.0, 0.0), (teams, LANES))


def answer_kernel(from_lower, from_upper, same, other, to_lower, to_upper):
    count, held_rows = same.shape[:2]
    teams = 2 * count
    mols = held_rows * LANES // FEAT
    half = CAP // 2
    names = []
    for asked in (from_lower, from_upper):
        names.append(asked[...].astype(jnp.float32).T)
    low = iota((LANES, LANES), 1) < FEAT - LANES
    mol = iota((CAP, mols), 1).astype(jnp.float32)
    for team in range(teams):
        held, at = (same, team) if team < count else (other, team - count)
        packed = held[at, mols:, :].astype(jnp.float32)
        turned = pltpu.roll(packed, FEAT - LANES, 1)
        rest = jnp.concatenate([jnp.where(low, packed, turned), jnp.where(low, turned, packed)], axis=0)
        values = jnp.concatenate([held[at, :mols, :], rest.astype(jnp.bfloat16)], axis=1)
        hits = []
        for side in range(2):
            column = team * KEYS + 2 - 2 * side
            name = names[side][:CAP, column : column + 1]
            hits.append((name == mol).astype(jnp.bfloat16))
        found = jnp.dot(jnp.concatenate(hits, axis=0), values, preferred_element_type=jnp.float32)
        for side, out in enumerate((to_lower, to_upper)):
            mine = found[side * CAP : (side + 1) * CAP]
            out[team, :CAP, :] = mine[:, :LANES].astype(jnp.bfloat16)
            pair = jnp.where(low[:half], mine[:half, LANES:], mine[half:, LANES:])
            out[team, CAP:, :] = pair.astype(jnp.bfloat16)


def owners(mols, first, per_mol, count):
    mol = (iota((1, BLOCK), 1) + first) // per_mol
    mol = jnp.where(mol < count, mol, -1)
    return (iota((mols, BLOCK), 0) == mol).astype(jnp.bfloat16)


def turned_kernel(per_mol, dest, info, guess, blocks, label, out, spare, mine, turned, slots, stage, rest, sems):
    step = pl.program_id(0)
    teams = out.shape[0]
    width = WIDTH

    @pl.when(step == 0)
    def _():
        turned[...] = jnp.zeros_like(turned)

        def clear(team, _):
            start = pl.multiple_of(team * width, width)
            for part in range(3):
                slots[part, pl.ds(start, width), :] = jnp.zeros((width, LANES), jnp.float32)
            return 0

        lax.fori_loop(0, teams, clear, 0)

    table = owners(guess.shape[1], step * BLOCK, per_mol, info[1])
    mine[...] = jnp.dot(guess[...], table, preferred_element_type=jnp.float32)

    def move(line):
        for first in range(0, LANES, MOVES):
            places = [dest[line + first + i] for i in range(MOVES)]
            rows = [
                [turned[part, first + i : first + i + 1, :] for part in range(3)]
                for i in range(MOVES)
            ]
            for place, row in zip(places, rows):
                for part in range(3):
                    slots[part, pl.ds(place, 1), :] = row[part]

    def column(at, _):
        cut = pl.ds(pl.multiple_of(at * LANES, LANES), LANES)
        move(jnp.maximum(step * BLOCK + (at - 1) * LANES, 0))
        results = []
        for side in range(2):
            sums = [[None] * 3 for _ in range(OCC)]
            for inner in range(BAS):
                first = (side * BAS + inner) * BAS
                block = [
                    blocks[first + 8 * g : first + 8 * g + 8, cut].astype(jnp.float32) for g in range(3)
                ]
                for k in range(OCC):
                    row = mine[inner * OCC + k : inner * OCC + k + 1, cut]
                    for g in range(3):
                        term = block[g] * row
                        sums[k][g] = term if inner == 0 else sums[k][g] + term
            results += [sums[k][g] for k in range(OCC) for g in range(3)]
        for part in range(3):
            turned[part] = jnp.concatenate(results[part * 16 : part * 16 + 16], axis=0).T

        return 0

    lax.fori_loop(0, BLOCK // LANES, column, 0)

    @pl.when(step == pl.num_programs(0) - 1)
    def _():
        move((step + 1) * BLOCK - LANES)

        def copies(team):
            peer = absolute(team, info[3])
            return [
                pltpu.make_async_copy(stage.at[team], out.at[peer], sems.at[0, team]),
                pltpu.make_async_copy(rest.at[team], spare.at[peer], sems.at[1, team]),
            ]

        def finish(team, _):
            start = pl.multiple_of(team * width, width)
            for part in range(3):
                stage[team, part * MAIN : (part + 1) * MAIN, :] = slots[
                    part, pl.ds(start, MAIN), :
                ].astype(jnp.bfloat16)
                rest[team, part * SPARE : (part + 1) * SPARE, :] = slots[
                    part, pl.ds(start + MAIN, SPARE), :
                ].astype(jnp.bfloat16)
            names = [label[row, pl.ds(team, 1), :] for row in range(7)]
            fill = jnp.zeros((16, LANES), jnp.float32)
            stage[team, 3 * MAIN :, :] = jnp.concatenate(names[:5] + [fill[5:]], axis=0).astype(
                jnp.bfloat16
            )
            rest[team, 3 * SPARE :, :] = jnp.concatenate(names[5:] + [fill[2:]], axis=0).astype(
                jnp.bfloat16
            )
            for copy in copies(team):
                copy.start()
            return 0

        def wait(team, _):
            for copy in copies(team):
                copy.wait()
            return 0

        lax.fori_loop(0, teams, finish, 0)
        lax.fori_loop(0, teams, wait, 0)


def apply_blocks(wide, theirs, applied, mine, cut):
    other = [theirs[OCC * b : OCC * b + OCC, :] for b in range(BAS)]
    reduced = [[None] * OCC for _ in range(2)]
    for a in range(BAS):
        for side in range(2):
            first = (side * BAS + a) * BAS
            total = None
            for b in range(BAS):
                term = wide[first + b : first + b + 1, :] * other[b]
                total = term if total is None else total + term
            row = (side * BAS + a) * OCC
            applied[row : row + OCC, cut] = total
            if mine is not None:
                for k in range(OCC):
                    term = mine[a * OCC + k : a * OCC + k + 1, cut] * total
                    reduced[side][k] = term if a == 0 else reduced[side][k] + term
    return reduced


def diagonal_kernel(guess, blocks, out, wide, mine):
    wide[...] = blocks[...].astype(jnp.float32)
    mine[...] = guess[...].astype(jnp.float32)
    apply_blocks(wide, mine, out, None, slice(0, LANES))


def pairs_kernel(
    per_mol, first_rows, rest_rows, info, guess, blocks, half, local, same, other, lower, upper, scores, total,
    wide, mine, theirs, applied, near_a, near_b, held,
):
    step = pl.program_id(0)
    mols = guess.shape[1]

    @pl.when(step == 0)
    def _():
        total[...] = local[...]

        base = 0
        for source in (same, other, lower, upper):
            rows = source.shape[1]

            def widen(team, _):
                start = pl.multiple_of(base + team * rows, rows)
                held[pl.ds(start, rows), :] = source[team].astype(jnp.float32)
                return 0

            lax.fori_loop(0, source.shape[0], widen, 0)
            base += source.shape[0] * rows

    table = owners(mols, step * BLOCK, per_mol, info[1])
    mine[...] = jnp.dot(guess[...], table, preferred_element_type=jnp.float32)

    def pick(line):
        for first in range(0, LANES, MOVES):
            for index, near in ((first_rows, near_a), (rest_rows, near_b)):
                places = [index[line * LANES + first + i] for i in range(MOVES)]
                rows = [held[pl.ds(place, 1), :] for place in places]
                near[first : first + MOVES, :] = jnp.concatenate(rows, axis=0)

    @pl.when(step == 0)
    def _():
        pick(0)

    def column(at, _):
        cut = pl.ds(pl.multiple_of(at * LANES, LANES), LANES)
        line = step * (BLOCK // LANES) + at
        theirs[:LANES, :] = near_a[...].T
        rest = near_b[...].T
        theirs[LANES:, :] = jnp.where(
            half[pl.ds(line, 1), :] > 0, rest[FEAT - LANES :], rest[: FEAT - LANES]
        )
        pick(jnp.minimum(line + 1, half.shape[0] - 1))
        wide[...] = blocks[:, cut].astype(jnp.float32)
        reduced = apply_blocks(wide, theirs, applied, mine, cut)
        scores[:, cut] = jnp.concatenate(reduced[0] + reduced[1], axis=0)
        return 0

    lax.fori_loop(0, BLOCK // LANES, column, 0)
    total[...] += lax.dot_general(
        applied[...].astype(jnp.bfloat16), table, NT, preferred_element_type=jnp.float32
    )


def tail_names(labels, low, high, mols):
    lane = iota((1, LANES), 1) // SPARE
    names = jnp.zeros((1, LANES), jnp.float32)
    for at, label in enumerate(labels):
        name = label[low : low + 1] + label[high : high + 1] * mols
        names = jnp.where(lane == at, name, names)
    return names


def collect_kernel(blocks, lower, here, upper, over, sums, flags):
    step = pl.program_id(0)
    mols = here.shape[0]

    @pl.when(step == 0)
    def _():
        sums[...] = jnp.zeros_like(sums)
        flags[...] = jnp.zeros_like(flags)

    peers = range(blocks.shape[0])
    labels = [blocks[i, 3 * MAIN :, :].astype(jnp.float32) for i in peers]
    names = [label[0:1] + label[2:3] * mols for label in labels]
    for first in range(0, len(labels), TAILS):
        names.append(tail_names(labels[first : first + TAILS], 1, 3, mols))
    names = jnp.concatenate(names, axis=1)
    mol = iota((SIDES * mols, names.shape[1]), 0).astype(jnp.float32)
    values = []
    for part in range(3):
        row = part * MAIN
        rows = [blocks[i, row : row + LANES, :] for i in peers]
        rows += [blocks[i, row + LANES : row + MAIN, :] for i in peers]
        values.append(jnp.concatenate(rows, axis=0))
    sums[...] += jnp.dot(
        (mol == names).astype(jnp.bfloat16),
        jnp.concatenate(values, axis=1),
        preferred_element_type=jnp.float32,
    )
    for label in labels:
        flags[...] = jnp.maximum(flags[...], label[:8])

    @pl.when(step == pl.num_programs(0) - 1)
    def _():
        for side, out in enumerate((lower, here, upper)):
            out[...] = sums[side * mols : (side + 1) * mols].astype(out.dtype)
        over[0] = (jnp.max(flags[4:5, :]) > 0).astype(jnp.int32)


def spare_kernel(blocks, lower, here, upper, lower_out, here_out, upper_out):
    mols = here.shape[0]
    teams = blocks.shape[0]
    names = []
    for first in range(0, teams, TAILS):
        labels = [
            blocks[i, 3 * SPARE :, :].astype(jnp.float32) for i in range(first, first + TAILS)
        ]
        names.append(tail_names(labels, 0, 1, mols))
    mol = iota((SIDES * mols, teams * SPARE), 0).astype(jnp.float32)
    values = []
    for part in range(3):
        row = part * SPARE
        values.append(
            jnp.concatenate([blocks[i, row : row + SPARE, :] for i in range(teams)], axis=0)
        )
    sums = jnp.dot(
        (mol == jnp.concatenate(names, axis=1)).astype(jnp.bfloat16),
        jnp.concatenate(values, axis=1),
        preferred_element_type=jnp.float32,
    )
    pairs = ((lower, lower_out), (here, here_out), (upper, upper_out))
    for side, (before, out) in enumerate(pairs):
        part = sums[side * mols : (side + 1) * mols]
        out[...] = (before[...].astype(jnp.float32) + part).astype(out.dtype)


def finish_kernel(info, total, here, from_lower, from_upper, out):
    mols = here.shape[0]
    back = here[...] + from_lower[...].astype(jnp.float32) + from_upper[...].astype(jnp.float32)
    high = back.astype(jnp.bfloat16)
    low = (back - high.astype(jnp.float32)).astype(jnp.bfloat16)
    row = iota((ROWS, ROWS), 0)
    column = iota((ROWS, ROWS), 1)
    turn = (column // FEAT) * FEAT + column % BAS * OCC + column % FEAT // BAS
    order = (row == turn).astype(jnp.bfloat16)
    returned = lax.dot_general(order, high, NT, preferred_element_type=jnp.float32)
    returned = returned + lax.dot_general(order, low, NT, preferred_element_type=jnp.float32)
    alive = iota((ROWS, mols), 1) < info[1]
    out[...] = jnp.where(alive, total[...] + returned, 0.0)


def shifted(block, axis, distance):
    devices = range(lax.axis_size(axis))
    route = [((i - distance) % len(devices), i) for i in devices]
    return lax.ppermute(block, axis, route)


def params(mib=48):
    return pltpu.CompilerParams(vmem_limit_bytes=mib * 1024 * 1024)


def cost(us):
    return pl.CostEstimate(flops=0, transcendentals=0, bytes_accessed=us * 3_600_000)


def on_device(history, diag_blocks, pair_blocks, neighbours, counts):
    mols = history.shape[2]
    pairs = pair_blocks.shape[1]
    per_mol = pairs // mols
    teams = lax.axis_size("sub")
    domains = lax.axis_size("dom")
    columns = pairs // LANES
    held_rows = mols * FEAT // LANES
    shape = jax.ShapeDtypeStruct
    f32, bf16, i32 = jnp.float32, jnp.bfloat16, jnp.int32
    info = jnp.stack([lax.axis_index("dom"), counts[0], lax.axis_index("sub") % 2, lax.axis_index("sub")]).astype(i32)
    guess, rows = pl.pallas_call(
        predict_kernel,
        out_shape=(shape((FEAT, mols), bf16), shape((CHIPS, held_rows, LANES), bf16)),
        in_specs=[VMEM],
        out_specs=(VMEM,) * 2,
        compiler_params=params(60),
        name="predict",
    )(history)

    table = shape((columns, LANES), i32)
    dest, first_rows, rest_rows, half, wanted, label = pl.pallas_call(
        functools.partial(rank_kernel, teams, domains, mols),
        out_shape=(table,) * 4 + (shape((teams * KEYS, LANES), i32), shape((7, teams, LANES), f32)),
        in_specs=[SMEM, VMEM],
        out_specs=(VMEM,) * 6,
        scratch_shapes=[
            pltpu.VMEM((columns * teams * (KEYS + 1), LANES), bf16),
            pltpu.VMEM((columns * teams * (KEYS + 1), 2 * LANES), f32),
            pltpu.VMEM((teams * KEYS, pairs), bf16),
            pltpu.VMEM((LANES, pairs), bf16),
            pltpu.VMEM((2 * teams, pairs), bf16),
            pltpu.VMEM((2 * LANES, pairs), bf16),
        ],
        compiler_params=params(60),
        cost_estimate=cost(3),
        name="rank",
    )(info, neighbours.reshape(columns, LANES))
    dest, first_rows, rest_rows = (x.reshape(pairs) for x in (dest, first_rows, rest_rows))

    cores = [[2 * chip + core for chip in range(CHIPS)] for core in range(2)]
    same = lax.all_to_all(rows, "sub", 0, 0, tiled=True, axis_index_groups=cores)
    asked_lower, asked_upper = shifted(wanted, "dom", 1), shifted(wanted, "dom", -1)

    payload, spare = pl.pallas_call(
        functools.partial(turned_kernel, per_mol),
        grid=(pairs // BLOCK,),
        out_shape=(
            shape((teams, 3 * MAIN + 16, LANES), bf16),
            shape((teams, 3 * SPARE + 16, LANES), bf16),
        ),
        in_specs=[
            SMEM,
            SMEM,
            pl.BlockSpec((FEAT, mols), lambda i: (0, 0)),
            pl.BlockSpec((6 * FEAT, BLOCK), lambda i: (0, i)),
            pl.BlockSpec((7, teams, LANES), lambda i: (0, 0, 0)),
        ],
        out_specs=(pl.BlockSpec(memory_space=pltpu.HBM),) * 2,
        scratch_shapes=[
            pltpu.VMEM((FEAT, BLOCK), f32),
            pltpu.VMEM((3, LANES, LANES), f32),
            pltpu.VMEM((3, teams * WIDTH, LANES), f32),
            pltpu.VMEM((teams, 3 * MAIN + 16, LANES), bf16),
            pltpu.VMEM((teams, 3 * SPARE + 16, LANES), bf16),
            pltpu.SemaphoreType.DMA((2, teams)),
        ],
        compiler_params=params(60),
        cost_estimate=cost(25),
        name="turned",
    )(dest, info, guess, pair_blocks, label)

    payload, same, asked_lower, asked_upper = lax.optimization_barrier(
        (payload, same, asked_lower, asked_upper)
    )
    received = lax.all_to_all(payload, "sub", 0, 0, tiled=True)

    other = lax.ppermute(same, "sub", [(i ^ 1, i) for i in range(teams)])
    to_lower, to_upper = pl.pallas_call(
        answer_kernel,
        out_shape=(shape((teams, PACKED, LANES), bf16),) * 2,
        in_specs=[VMEM] * 4,
        out_specs=(VMEM,) * 2,
        compiler_params=params(),
        name="answer",
    )(asked_lower, asked_upper, same, other)
    upper = shifted(to_lower, "dom", -1)
    lower = shifted(to_upper, "dom", 1)

    local = pl.pallas_call(
        diagonal_kernel,
        grid=(mols // LANES,),
        out_shape=shape((ROWS, mols), f32),
        in_specs=[
            pl.BlockSpec((FEAT, LANES), lambda i: (0, i)),
            pl.BlockSpec((6 * FEAT, LANES), lambda i: (0, i)),
        ],
        out_specs=pl.BlockSpec((ROWS, LANES), lambda i: (0, i)),
        scratch_shapes=[
            pltpu.VMEM((6 * FEAT, LANES), f32),
            pltpu.VMEM((FEAT, LANES), f32),
        ],
        compiler_params=params(),
        name="diagonal",
    )(guess, diag_blocks)

    scores, total = pl.pallas_call(
        functools.partial(pairs_kernel, per_mol),
        grid=(pairs // BLOCK,),
        out_shape=(shape((ROWS // 3, pairs), f32), shape((ROWS, mols), f32)),
        in_specs=[
            SMEM,
            SMEM,
            SMEM,
            pl.BlockSpec((FEAT, mols), lambda i: (0, 0)),
            pl.BlockSpec((6 * FEAT, BLOCK), lambda i: (0, i)),
            pl.BlockSpec((columns, LANES), lambda i: (0, 0)),
            pl.BlockSpec((ROWS, mols), lambda i: (0, 0)),
            pl.BlockSpec((teams // 2, held_rows, LANES), lambda i: (0, 0, 0)),
            pl.BlockSpec((teams // 2, held_rows, LANES), lambda i: (0, 0, 0)),
            pl.BlockSpec((teams, PACKED, LANES), lambda i: (0, 0, 0)),
            pl.BlockSpec((teams, PACKED, LANES), lambda i: (0, 0, 0)),
        ],
        out_specs=(
            pl.BlockSpec((ROWS // 3, BLOCK), lambda i: (0, i)),
            pl.BlockSpec((ROWS, mols), lambda i: (0, 0)),
        ),
        scratch_shapes=[
            pltpu.VMEM((6 * FEAT, LANES), f32),
            pltpu.VMEM((FEAT, BLOCK), f32),
            pltpu.VMEM((FEAT, LANES), f32),
            pltpu.VMEM((ROWS, BLOCK), f32),
            pltpu.VMEM((LANES, LANES), f32),
            pltpu.VMEM((LANES, LANES), f32),
            pltpu.VMEM((teams * (held_rows + 2 * PACKED), LANES), f32),
        ],
        compiler_params=params(),
        cost_estimate=cost(35),
        name="pairs",
    )(first_rows, rest_rows, info, guess, pair_blocks, half, local, same, other, lower, upper)

    received, total = lax.optimization_barrier((received, total))
    whole = pl.BlockSpec((mols, ROWS), lambda i: (0, 0))
    group = 8
    sums_shape = (shape((mols, ROWS), bf16), shape((mols, ROWS), f32), shape((mols, ROWS), bf16))
    below, here, above, over = pl.pallas_call(
        collect_kernel,
        grid=(teams // group,),
        out_shape=sums_shape + (shape((1,), i32),),
        in_specs=[pl.BlockSpec((group, 3 * MAIN + 16, LANES), lambda i: (i, 0, 0))],
        out_specs=(whole,) * 3 + (SMEM,),
        scratch_shapes=[pltpu.VMEM((SIDES * mols, ROWS), f32), pltpu.VMEM((8, LANES), f32)],
        compiler_params=params(),
        name="collect",
    )(received)

    def second_round(spare, *sums):
        rest = lax.all_to_all(spare, "sub", 0, 0, tiled=True)
        return pl.pallas_call(
            spare_kernel,
            out_shape=sums_shape,
            in_specs=[VMEM] * 4,
            out_specs=(VMEM,) * 3,
            compiler_params=params(),
            name="spare",
        )(rest, *sums)

    below, here, above = lax.cond(
        over[0] > 0, second_round, lambda spare, *sums: sums, spare, below, here, above
    )
    from_lower, from_upper = shifted(above, "dom", 1), shifted(below, "dom", -1)

    products = pl.pallas_call(
        finish_kernel,
        out_shape=shape((ROWS, mols), f32),
        in_specs=[SMEM] + [VMEM] * 4,
        out_specs=VMEM,
        compiler_params=params(),
        name="finish",
    )(info, total, here, from_lower, from_upper)
    return products, scores


def solution(mesh):
    in_specs = (
        P(None, None, ("dom", "sub")),
        P(None, ("dom", "sub")),
        P(None, ("dom", "sub")),
        P(("dom", "sub")),
        P(("dom", "sub")),
    )
    out_specs = (P(None, ("dom", "sub")), P(None, ("dom", "sub")))
    return jax.shard_map(
        on_device, mesh=mesh, in_specs=in_specs, out_specs=out_specs, check_vma=False
    )
```
